256 devices in a mesh: section: 16 (over x, z_lo), dp: 16 (over z_hi, y, core).
Axes of the slice: x: 4, y: 4, z: 8 (z_hi: 2, z_lo: 4; z = z_hi * 4 + z_lo), core: 2. Of those that a mesh axis runs over, the one named last changes fastest.
Arguments:
- stream_in: bfloat16 [4096, 2048], P('dp'), may hold values from -6 to 6
- sample_ids: int32 [16, 8], P('dp'), may hold values from 0 to 31
- epoch_buffer: bfloat16 [16, 512, 32, 2048], P('section', 'dp'), may hold values from -8 to 8
- layer_weight: bfloat16 [16, 2048, 2048], P('section', 'dp'), may hold values from -0.125 to 0.125
- top_cotangent: bfloat16 [4096, 2048], P('dp'), may hold values from -6 to 6
Outputs:
- decoded: bfloat16 [16, 4096, 2048], P('section', 'dp')
- weight_grad: float32 [16, 2048, 2048], P('section', 'dp')
The draws below stay inside these ranges and needn't reach their ends.
Inputs may be any that keep to these rules, and one draw needn't show every extreme that they name: `sample_ids`: an entry of the replica's own pool of 32 samples.
All inputs are finite; a program needn't handle non-finite values.
Results may differ from the reference program's by a relative error of at most 0.035.
Values may be sent and summed in bfloat16 or wider, within the bound.
No kernel may reach another device: no remote copies, remote signals or barrier semaphores. Data moves between devices by JAX's collectives and lax.ppermute only.
A program may use at most 128 MiB of HBM per device.

```python
import jax
import jax.numpy as jnp
from jax import lax

D = 2048
SECTIONS = 16
MB = 8
TOK_MB = 32
POOL = 32
ROWS = 4096
N_DP = 16


def touch_ends(result, rng, low, top_value):
    longest = result.shape.index(max(result.shape))
    spots = []
    for shift in (0, 1):
        where = [jax.random.randint(jax.random.fold_in(rng, axis), (), 0, length) for axis, length in enumerate(result.shape)]
        where[longest] = (where[longest] + shift) % result.shape[longest]
        spots.append(tuple(where))
    return result.at[spots[0]].set(low).at[spots[1]].set(top_value)


def block_levels(own_key, dims, cuts, smallest, top_value):
    factor_of = 1.0
    for dim, blocks in cuts:
        steps = jax.random.uniform(jax.random.fold_in(jax.random.fold_in(own_key, 6), dim), (blocks,), jnp.float32, smallest / len(cuts), top_value / len(cuts))
        factor_of = factor_of * jnp.repeat(jnp.exp(steps), dims[dim] // blocks).reshape((-1,) + (1,) * (len(dims) - 1 - dim))
    return factor_of


def normal_values(rng, shape, deviation, limit, shards=(), kind=jnp.bfloat16):
    result = jax.random.normal(rng, shape, jnp.float32) * deviation
    if len(shards) > 0:
        result = block_levels(rng, shape, shards, -0.22, 0.18) * result
    return jnp.clip(result, min=-limit, max=limit).astype(kind)


def setup_inputs(seed: int = 0) -> dict:
    seeds = jax.random.split(jax.random.key(seed), 6)
    stream_in = normal_values(seeds[0], (ROWS, D), 1.0, 6.0, ((0, 16),))
    sample_ids = touch_ends(jax.random.randint(seeds[1], (N_DP, MB), 0, POOL), jax.random.fold_in(seeds[1], 1), 0, POOL - 1).astype(jnp.int32)
    epoch_buffer = normal_values(seeds[2], (SECTIONS, N_DP * POOL, TOK_MB, D), 1.5, 8.0, ((0, 16), (1, 16)))
    layer_weight = normal_values(seeds[3], (SECTIONS, D, D), D ** -0.5, 0.125, ((0, 16), (1, 16)))
    top_cotangent = normal_values(seeds[4], (ROWS, D), 1.0, 6.0, ((0, 16),))
    return dict(stream_in=stream_in, sample_ids=sample_ids, epoch_buffer=epoch_buffer, layer_weight=layer_weight, top_cotangent=top_cotangent)


epsilon = 1e-05

def normalize(values):
    return values * lax.rsqrt(lax.optimization_barrier(jnp.mean(values * values, axis=-1, keepdims=True)) + epsilon)

def encode(output_rows, base_rows):
    bound_rows = 2.0 * jnp.sqrt(lax.optimization_barrier(jnp.mean(output_rows * output_rows, axis=-1, keepdims=True)) + epsilon)
    delta_rows = jnp.clip(output_rows - base_rows, -bound_rows, bound_rows).astype(jnp.bfloat16)
    return (base_rows + delta_rows.astype(jnp.float32)).astype(jnp.bfloat16)

def reference(stream_in, sample_ids, epoch_buffer, layer_weight, top_cotangent):
    replicas = sample_ids.shape[0]
    replica_rows = jnp.arange(replicas, dtype=jnp.int32)[:, None]
    current = stream_in
    inputs_kept = []
    decoded_all = []
    for layer in range(SECTIONS):
        stored = epoch_buffer[layer].reshape(replicas, POOL, TOK_MB, D)
        base_rows = stored[replica_rows, sample_ids].reshape(-1, D).astype(jnp.float32)
        inputs_kept.append(current)
        values = current.astype(jnp.float32)
        normed = normalize(values).astype(jnp.bfloat16)
        output_rows = values + jnp.dot(normed, layer_weight[layer], preferred_element_type=jnp.float32)
        current = encode(output_rows, base_rows)
        decoded_all.append(current)
    cotangent = top_cotangent
    gradients = [None] * SECTIONS
    for layer in range(SECTIONS - 1, -1, -1):
        values = inputs_kept[layer].astype(jnp.float32)
        normed = normalize(values).astype(jnp.bfloat16)
        per_replica = jnp.einsum('rti,rto->rio', normed.reshape(replicas, -1, D).astype(jnp.float32), cotangent.reshape(replicas, -1, D).astype(jnp.float32), precision=lax.Precision.HIGHEST)
        rounded = lax.optimization_barrier(per_replica.astype(jnp.bfloat16))
        gradients[layer] = lax.optimization_barrier(jnp.sum(rounded.astype(jnp.float32), axis=0))
        backward_rows = lax.dot_general(cotangent, layer_weight[layer], (((1,), (1,)), ((), ())), preferred_element_type=jnp.float32)
        through = jax.vjp(normalize, values)[1](backward_rows)[0]
        cotangent = (cotangent.astype(jnp.float32) + through).astype(jnp.bfloat16)
    return (jnp.stack(decoded_all), jnp.stack(gradients))
```

```python
import functools

import jax
import jax.numpy as jnp
from jax import lax
from jax.experimental import pallas as pl
from jax.experimental.pallas import tpu as pltpu
from jax.sharding import Mesh
from jax.sharding import PartitionSpec as P

epsilon = 1e-05
STAGES = 4
DEPTH = 4
TILE = 512
PLANE = ("zl", "zh", "y", "c")


def forward_kernel(x_ref, base_ref, w_ref, out_ref, x_now, normed, y):
    layer, tile = pl.program_id(0), pl.program_id(1)
    tiles = pl.num_programs(1)

    @pl.when((layer == 0) & (tile == 0))
    def _():
        x_now[...] = x_ref[...].astype(jnp.float32)

    @pl.when(tile == 0)
    def _():
        values = x_now[...]
        scale = lax.rsqrt(jnp.mean(values * values, axis=-1, keepdims=True) + epsilon)
        normed[...] = (values * scale).astype(jnp.bfloat16)

    columns = pl.ds(pl.multiple_of(tile * TILE, TILE), TILE)
    y[:, columns] = x_now[:, columns] + jnp.dot(
        normed[...], w_ref[0], preferred_element_type=jnp.float32
    )

    @pl.when(tile == tiles - 1)
    def _():
        rows = y[...]
        base = base_ref[0].astype(jnp.float32)
        bound = 2.0 * jnp.sqrt(jnp.mean(rows * rows, axis=-1, keepdims=True) + epsilon)
        delta = jnp.clip(rows - base, -bound, bound).astype(jnp.bfloat16)
        coded = (base + delta.astype(jnp.float32)).astype(jnp.bfloat16)
        out_ref[0] = coded
        x_now[...] = coded.astype(jnp.float32)


def forward_stage(x, base, weight):
    depth, rows, width = base.shape
    return pl.pallas_call(
        forward_kernel,
        grid=(depth, width // TILE),
        in_specs=[
            pl.BlockSpec((rows, width), lambda i, j: (0, 0)),
            pl.BlockSpec((1, rows, width), lambda i, j: (i, 0, 0)),
            pl.BlockSpec((1, width, TILE), lambda i, j: (i, 0, j)),
        ],
        out_specs=pl.BlockSpec((1, rows, width), lambda i, j: (i, 0, 0)),
        out_shape=jax.ShapeDtypeStruct((depth, rows, width), jnp.bfloat16),
        scratch_shapes=[
            pltpu.VMEM((rows, width), jnp.float32),
            pltpu.VMEM((rows, width), jnp.bfloat16),
            pltpu.VMEM((rows, width), jnp.float32),
        ],
        compiler_params=pltpu.CompilerParams(vmem_limit_bytes=32 * 1024 * 1024),
        cost_estimate=pl.CostEstimate(
            flops=2 * depth * rows * width * width,
            bytes_accessed=2 * depth * width * width,
            transcendentals=0,
        ),
    )(x, base, weight)


def backward_kernel(g_ref, x_ref, w_ref, seen_ref, out_ref, g_now, back):
    step, tile = pl.program_id(0), pl.program_id(1)
    tiles = pl.num_programs(1)

    @pl.when((step == 0) & (tile == 0))
    def _():
        g_now[...] = g_ref[...]

    columns = pl.ds(pl.multiple_of(tile * TILE, TILE), TILE)
    back[:, columns] = lax.dot_general(
        g_now[...], w_ref[0], (((1,), (1,)), ((), ())), preferred_element_type=jnp.float32
    )

    @pl.when(tile == tiles - 1)
    def _():
        values = x_ref[0].astype(jnp.float32)
        scale = lax.rsqrt(jnp.mean(values * values, axis=-1, keepdims=True) + epsilon)
        through = back[...]
        along = jnp.mean(values * scale * through, axis=-1, keepdims=True)
        seen_ref[0] = g_now[...]
        sent = g_now[...].astype(jnp.float32) + scale * (through - values * scale * along)
        sent = sent.astype(jnp.bfloat16)
        g_now[...] = sent
        out_ref[...] = sent


def backward_stage(g, x, weight):
    depth, rows, width = x.shape
    last = depth - 1
    return pl.pallas_call(
        backward_kernel,
        grid=(depth, width // TILE),
        in_specs=[
            pl.BlockSpec((rows, width), lambda i, j: (0, 0)),
            pl.BlockSpec((1, rows, width), lambda i, j: (last - i, 0, 0)),
            pl.BlockSpec((1, TILE, width), lambda i, j: (last - i, j, 0)),
        ],
        out_specs=[
            pl.BlockSpec((1, rows, width), lambda i, j: (last - i, 0, 0)),
            pl.BlockSpec((rows, width), lambda i, j: (0, 0)),
        ],
        out_shape=[
            jax.ShapeDtypeStruct((depth, rows, width), jnp.bfloat16),
            jax.ShapeDtypeStruct((rows, width), jnp.bfloat16),
        ],
        scratch_shapes=[
            pltpu.VMEM((rows, width), jnp.bfloat16),
            pltpu.VMEM((rows, width), jnp.float32),
        ],
        compiler_params=pltpu.CompilerParams(vmem_limit_bytes=32 * 1024 * 1024),
        cost_estimate=pl.CostEstimate(
            flops=2 * depth * rows * width * width,
            bytes_accessed=2 * depth * width * width,
            transcendentals=0,
        ),
    )(g, x, weight)


def shift(value, axis, steps):
    count = lax.axis_size(axis)
    return lax.ppermute(value, axis, [(i, (i + steps) % count) for i in range(count)])


def exchange(value):
    return lax.all_to_all(value, "zl", 0, 0)


def gradient_sum(normed, g):
    rows, width = normed.shape
    core, y, zh = lax.axis_index("c"), lax.axis_index("y"), lax.axis_index("zh")
    chips = lax.axis_size("zh") * lax.axis_size("y")
    piece = width // (2 * chips)
    by_core = normed.reshape(rows, chips, 2, piece)
    mine = lax.dynamic_index_in_dim(by_core, core, 2, keepdims=False).reshape(rows, -1)
    theirs = lax.dynamic_index_in_dim(by_core, 1 - core, 2, keepdims=False).reshape(rows, -1)
    left = jnp.concatenate([mine, shift(theirs, "c", 1)], axis=0)
    right = jnp.concatenate([g, shift(g, "c", 1)], axis=0)

    left = left.reshape(2 * rows, 2, 4, piece)

    def block(steps):
        picked = lax.dynamic_index_in_dim(left, lax.rem(y + steps + 4, 4), 2, keepdims=False)
        return lax.dot_general(
            picked.reshape(2 * rows, 2 * piece), right, (((0,), (0,)), ((), ())),
            preferred_element_type=jnp.float32,
        )

    half = width // 2
    far = block(2).astype(jnp.bfloat16)
    up1 = shift(far[:, :half], "y", 1)
    down1 = shift(far[:, half:], "y", -1)
    up, down, own = block(1), block(-1), block(0)
    up = jnp.concatenate([up[:, :half] + up1.astype(jnp.float32), up[:, half:]], axis=1)
    down = jnp.concatenate([down[:, :half], down[:, half:] + down1.astype(jnp.float32)], axis=1)
    up2 = shift(up.astype(jnp.bfloat16), "y", 1)
    down2 = shift(down.astype(jnp.bfloat16), "y", -1)
    total = own + up2.astype(jnp.float32) + down2.astype(jnp.float32)
    total = total.reshape(2, piece, width)
    kept = lax.dynamic_index_in_dim(total, zh, 0, keepdims=False)
    given = lax.dynamic_index_in_dim(total, 1 - zh, 0, keepdims=False).astype(jnp.bfloat16)
    return kept + shift(given, "zh", 1).astype(jnp.float32)


def local(stream_in, sample_ids, epoch_buffer, layer_weight, top_cotangent):
    stage, lane = lax.axis_index("x"), lax.axis_index("zl")
    width = stream_in.shape[1]
    rows = stream_in.shape[0] // DEPTH
    weight = lax.all_gather(layer_weight[0], PLANE, axis=0, tiled=True)
    weight = weight.reshape(DEPTH, width, width)
    picked = jnp.take(epoch_buffer[0], sample_ids[0], axis=0)
    base = exchange(picked.reshape(DEPTH, rows, width))
    x = lax.dynamic_slice_in_dim(stream_in, lane * rows, rows, 0)
    g = lax.dynamic_slice_in_dim(top_cotangent, lane * rows, rows, 0)

    decoded = forward_stage(x, base, weight)
    for t in range(1, STAGES):
        arrived = lax.ppermute(decoded[DEPTH - 1], "x", [(t - 1, t)])
        x = jnp.where(stage == t, arrived, x)
        decoded = lax.cond(
            stage == t, lambda a, d: forward_stage(a, base, weight), lambda a, d: d, x, decoded
        )
    inputs = jnp.concatenate([x[None], decoded[: DEPTH - 1]], axis=0)

    seen, sent = backward_stage(g, inputs, weight)
    for t in range(STAGES - 2, -1, -1):
        arrived = lax.ppermute(sent, "x", [(t + 1, t)])
        g = jnp.where(stage == t, arrived, g)
        seen, sent = lax.cond(
            stage == t,
            lambda a, s, o: tuple(backward_stage(a, inputs, weight)),
            lambda a, s, o: (s, o),
            g, seen, sent,
        )

    decoded_rows = exchange(decoded).reshape(1, DEPTH * rows, width)
    input_rows = exchange(inputs).reshape(DEPTH * rows, width).astype(jnp.float32)
    scale = lax.rsqrt(jnp.mean(input_rows * input_rows, axis=-1, keepdims=True) + epsilon)
    normed = (input_rows * scale).astype(jnp.bfloat16)
    cotangents = exchange(seen).reshape(DEPTH * rows, width)
    return decoded_rows, gradient_sum(normed, cotangents)[None]


def solution(mesh):
    fine = Mesh(mesh.devices.reshape(4, 4, 2, 4, 2), ("x", "zl", "zh", "y", "c"))
    section, dp = ("x", "zl"), ("zh", "y", "c")
    in_specs = (
        P(dp, None),
        P(dp, None),
        P(section, dp, None, None),
        P(section, dp, None),
        P(dp, None),
    )
    out_specs = (P(section, dp, None), P(section, dp, None))
    return jax.shard_map(local, mesh=fine, in_specs=in_specs, out_specs=out_specs, check_vma=False)
```

```python
import functools

import jax
import jax.numpy as jnp
from jax import lax
from jax.experimental import pallas as pl
from jax.experimental.pallas import tpu as pltpu
from jax.sharding import Mesh
from jax.sharding import PartitionSpec as P

epsilon = 1e-05
STAGES = 4
DEPTH = 4
TILE = 512
SLOTS = 8
PLANE = ("zl", "zh", "y", "c")


def tile_copies(w_ref, held, arrived, depth, tiles, order, by_rows):
    slots = held.shape[0]

    def copy(number):
        slot = lax.rem(number, slots)
        layer = order(number // tiles)
        span = pl.ds(pl.multiple_of(lax.rem(number, tiles) * TILE, TILE), TILE)
        source = w_ref.at[layer, span] if by_rows else w_ref.at[layer, :, span]
        return pltpu.make_async_copy(source, held.at[slot], arrived.at[slot])

    def refill(number):
        @pl.when(number + slots < depth * tiles)
        def _():
            copy(number + slots).start()

    for number in range(slots):
        copy(jnp.int32(number)).start()
    return copy, refill


def forward_kernel(x_ref, base_ref, w_ref, out_ref, x_now, normed, y, held, arrived):
    depth, rows, width = base_ref.shape
    tiles, slots = width // TILE, held.shape[0]
    copy, refill = tile_copies(w_ref, held, arrived, depth, tiles, lambda i: i, False)
    x_now[...] = x_ref[...].astype(jnp.float32)

    def run_layer(layer, carry):
        values = x_now[...]
        scale = lax.rsqrt(jnp.mean(values * values, axis=-1, keepdims=True) + epsilon)
        normed[...] = (values * scale).astype(jnp.bfloat16)
        for tile in range(tiles):
            number = layer * tiles + tile
            copy(number).wait()
            columns = pl.ds(tile * TILE, TILE)
            y[:, columns] = x_now[:, columns] + jnp.dot(
                normed[...], held[lax.rem(number, slots)], preferred_element_type=jnp.float32
            )
            refill(number)
        values = y[...]
        base = base_ref[layer].astype(jnp.float32)
        bound = 2.0 * jnp.sqrt(jnp.mean(values * values, axis=-1, keepdims=True) + epsilon)
        delta = jnp.clip(values - base, -bound, bound).astype(jnp.bfloat16)
        coded = (base + delta.astype(jnp.float32)).astype(jnp.bfloat16)
        out_ref[layer] = coded
        x_now[...] = coded.astype(jnp.float32)
        return carry

    lax.fori_loop(0, depth, run_layer, 0)


def backward_kernel(g_ref, x_ref, w_ref, seen_ref, out_ref, g_now, back, held, arrived):
    depth, rows, width = x_ref.shape
    tiles, slots = width // TILE, held.shape[0]
    copy, refill = tile_copies(w_ref, held, arrived, depth, tiles, lambda i: depth - 1 - i, True)
    g_now[...] = g_ref[...]

    def run_layer(step, carry):
        layer = depth - 1 - step
        seen_ref[layer] = g_now[...]
        for tile in range(tiles):
            number = step * tiles + tile
            copy(number).wait()
            back[:, pl.ds(tile * TILE, TILE)] = lax.dot_general(
                g_now[...], held[lax.rem(number, slots)], (((1,), (1,)), ((), ())),
                preferred_element_type=jnp.float32,
            )
            refill(number)
        values = x_ref[layer].astype(jnp.float32)
        scale = lax.rsqrt(jnp.mean(values * values, axis=-1, keepdims=True) + epsilon)
        normed = values * scale
        through = back[...]
        along = jnp.mean(normed * through, axis=-1, keepdims=True)
        sent = g_now[...].astype(jnp.float32) + scale * (through - normed * along)
        g_now[...] = sent.astype(jnp.bfloat16)
        return carry

    lax.fori_loop(0, depth, run_layer, 0)
    out_ref[...] = g_now[...]


def stage_call(kernel, tile_shape, scratch, outs, depth, rows, width):
    vmem = pl.BlockSpec(memory_space=pltpu.VMEM)
    return pl.pallas_call(
        kernel,
        in_specs=[vmem, vmem, pl.BlockSpec(memory_space=pl.ANY)],
        out_specs=[vmem] * len(outs),
        out_shape=[jax.ShapeDtypeStruct(shape, jnp.bfloat16) for shape in outs],
        scratch_shapes=[
            *scratch,
            pltpu.VMEM((SLOTS, *tile_shape), jnp.bfloat16),
            pltpu.SemaphoreType.DMA((SLOTS,)),
        ],
        compiler_params=pltpu.CompilerParams(vmem_limit_bytes=32 * 1024 * 1024),
        cost_estimate=pl.CostEstimate(
            flops=2 * depth * rows * width * width,
            bytes_accessed=2 * depth * width * width,
            transcendentals=0,
        ),
    )


def forward_stage(x, base, weight):
    depth, rows, width = base.shape
    scratch = [
        pltpu.VMEM((rows, width), jnp.float32),
        pltpu.VMEM((rows, width), jnp.bfloat16),
        pltpu.VMEM((rows, width), jnp.float32),
    ]
    call = stage_call(
        forward_kernel, (width, TILE), scratch, [(depth, rows, width)], depth, rows, width
    )
    return call(x, base, weight)[0]


def backward_stage(g, x, weight):
    depth, rows, width = x.shape
    scratch = [pltpu.VMEM((rows, width), jnp.bfloat16), pltpu.VMEM((rows, width), jnp.float32)]
    outs = [(depth, rows, width), (rows, width)]
    call = stage_call(backward_kernel, (TILE, width), scratch, outs, depth, rows, width)
    return call(g, x, weight)


def shift(value, axis, steps):
    count = lax.axis_size(axis)
    return lax.ppermute(value, axis, [(i, (i + steps) % count) for i in range(count)])


def exchange(value):
    return lax.all_to_all(value, "zl", 0, 0)


def gradient_sum(normed, g):
    rows, width = normed.shape
    core, y, zh = lax.axis_index("c"), lax.axis_index("y"), lax.axis_index("zh")
    chips = lax.axis_size("zh") * lax.axis_size("y")
    piece = width // (2 * chips)
    by_core = normed.reshape(rows, chips, 2, piece)
    mine = lax.dynamic_index_in_dim(by_core, core, 2, keepdims=False).reshape(rows, -1)
    theirs = lax.dynamic_index_in_dim(by_core, 1 - core, 2, keepdims=False).reshape(rows, -1)
    left = jnp.concatenate([mine, shift(theirs, "c", 1)], axis=0)
    right = jnp.concatenate([g, shift(g, "c", 1)], axis=0)

    left = left.reshape(2 * rows, 2, 4, piece)

    def block(steps):
        picked = lax.dynamic_index_in_dim(left, lax.rem(y + steps + 4, 4), 2, keepdims=False)
        return lax.dot_general(
            picked.reshape(2 * rows, 2 * piece), right, (((0,), (0,)), ((), ())),
            preferred_element_type=jnp.float32,
        )

    half = width // 2
    far = block(2).astype(jnp.bfloat16)
    up1 = shift(far[:, :half], "y", 1)
    down1 = shift(far[:, half:], "y", -1)
    up, down, own = block(1), block(-1), block(0)
    up = jnp.concatenate([up[:, :half] + up1.astype(jnp.float32), up[:, half:]], axis=1)
    down = jnp.concatenate([down[:, :half], down[:, half:] + down1.astype(jnp.float32)], axis=1)
    up2 = shift(up.astype(jnp.bfloat16), "y", 1)
    down2 = shift(down.astype(jnp.bfloat16), "y", -1)
    total = own + up2.astype(jnp.float32) + down2.astype(jnp.float32)
    total = total.reshape(2, piece, width)
    kept = lax.dynamic_index_in_dim(total, zh, 0, keepdims=False)
    given = lax.dynamic_index_in_dim(total, 1 - zh, 0, keepdims=False).astype(jnp.bfloat16)
    return kept + shift(given, "zh", 1).astype(jnp.float32)


def local(stream_in, sample_ids, epoch_buffer, layer_weight, top_cotangent):
    stage, lane = lax.axis_index("x"), lax.axis_index("zl")
    width = stream_in.shape[1]
    rows = stream_in.shape[0] // DEPTH
    weight = lax.all_gather(layer_weight[0], PLANE, axis=0, tiled=True)
    weight = weight.reshape(DEPTH, width, width)
    picked = jnp.take(epoch_buffer[0], sample_ids[0], axis=0)
    base = exchange(picked.reshape(DEPTH, rows, width))
    x = lax.dynamic_slice_in_dim(stream_in, lane * rows, rows, 0)
    g = lax.dynamic_slice_in_dim(top_cotangent, lane * rows, rows, 0)

    decoded = forward_stage(x, base, weight)
    for t in range(1, STAGES):
        arrived = lax.ppermute(decoded[DEPTH - 1], "x", [(t - 1, t)])
        x = jnp.where(stage == t, arrived, x)
        decoded = lax.cond(
            stage == t, lambda a, d: forward_stage(a, base, weight), lambda a, d: d, x, decoded
        )
    inputs = jnp.concatenate([x[None], decoded[: DEPTH - 1]], axis=0)

    seen, sent = backward_stage(g, inputs, weight)
    for t in range(STAGES - 2, -1, -1):
        arrived = lax.ppermute(sent, "x", [(t + 1, t)])
        g = jnp.where(stage == t, arrived, g)
        seen, sent = lax.cond(
            stage == t,
            lambda a, s, o: tuple(backward_stage(a, inputs, weight)),
            lambda a, s, o: (s, o),
            g, seen, sent,
        )

    decoded_rows = exchange(decoded).reshape(1, DEPTH * rows, width)
    input_rows = exchange(inputs).reshape(DEPTH * rows, width).astype(jnp.float32)
    scale = lax.rsqrt(jnp.mean(input_rows * input_rows, axis=-1, keepdims=True) + epsilon)
    normed = (input_rows * scale).astype(jnp.bfloat16)
    cotangents = exchange(seen).reshape(DEPTH * rows, width)
    return decoded_rows, gradient_sum(normed, cotangents)[None]


def solution(mesh):
    fine = Mesh(mesh.devices.reshape(4, 4, 2, 4, 2), ("x", "zl", "zh", "y", "c"))
    section, dp = ("x", "zl"), ("zh", "y", "c")
    in_specs = (
        P(dp, None),
        P(dp, None),
        P(section, dp, None, None),
        P(section, dp, None),
        P(dp, None),
    )
    out_specs = (P(section, dp, None), P(section, dp, None))
    return jax.shard_map(local, mesh=fine, in_specs=in_specs, out_specs=out_specs, check_vma=False)
```

```python
import functools

import jax
import jax.numpy as jnp
from jax import lax
from jax.experimental import pallas as pl
from jax.experimental.pallas import tpu as pltpu
from jax.sharding import Mesh
from jax.sharding import PartitionSpec as P

epsilon = 1e-05
STAGES = 4
DEPTH = 4
SLOTS = 2


def shift(value, axis, steps):
    count = lax.axis_size(axis)
    return lax.ppermute(value, axis, [(i, (i + steps) % count) for i in range(count)])


def shift_z(value, steps):
    lows, highs = lax.axis_size("zl"), lax.axis_size("zh")
    spot = [(z % lows) * highs + z // lows for z in range(lows * highs)]
    count = len(spot)
    return lax.ppermute(
        value, ("zl", "zh"), [(spot[z], spot[(z + steps) % count]) for z in range(count)]
    )


def gather_pieces(shard):
    split = shard.shape[1] * 5 // 8
    half = shard.shape[0] // 2
    one, two = shard[:, :split], shard[:, split:]
    pieces = []

    below, above = shift(two, "y", 1), shift(two, "y", -1)
    column = jnp.stack([two, below, above, shift(below, "y", 1)])
    offsets = (0, 3, 1, 2)

    m1, p1 = shift_z(one, 1), shift_z(one, -1)
    m2, p2 = shift_z(m1, 1), shift_z(p1, -1)
    m3, p3 = shift_z(m2, 1), shift_z(p2, -1)
    m4 = shift_z(m3, 1)
    for units, zs in (((one, m1, p1), (0, 7, 1)), ((m2, p2, m3, p3, m4), (6, 2, 5, 3, 4))):
        batch = jnp.stack(units)
        below, above = shift(batch, "y", 1), shift(batch, "y", -1)
        far_low = shift(below[:, :half], "y", 1)
        far_high = shift(above[:, half:], "y", -1)
        for array, first, y in (
            (batch, 0, 0), (below, 0, 3), (above, 0, 1), (far_low, 0, 2), (far_high, half, 2)
        ):
            pieces.append((0, array, first, zs, (y,) * len(zs)))

    pieces.append((1, column, 0, (0,) * 4, offsets))
    low = high = column
    for z in (1, 2, 3, 4):
        high = shift_z(high, -1)
        pieces.append((1, high, 0, (z,) * 4, offsets))
        if z < 4:
            low = shift_z(low, 1)
            pieces.append((1, low, 0, (8 - z,) * 4, offsets))
    arrays = [[array, shift(array, "c", 1)] for _, array, _, _, _ in pieces]
    plan = [(part, first, zs, ys) for part, _, first, zs, ys in pieces]
    return arrays, plan


def layer_copies(plan, refs, held, arrived, order):
    lane, zh = lax.axis_index("zl"), lax.axis_index("zh")
    y, core = lax.axis_index("y"), lax.axis_index("c")
    depth = DEPTH
    piece = held[0].shape[1] // 16
    slots = held[0].shape[0]

    def start(step, part):
        slot = lax.rem(step, slots)
        nearest = lax.rem(order(step) - lane + depth, depth)
        for offset in range(depth):

            @pl.when(nearest == offset)
            def _(offset=offset):
                for index, (kind, first, zs, ys) in enumerate(plan):
                    for unit, (dz, dy) in enumerate(zip(zs, ys)):
                        if kind != part or dz % depth != offset:
                            continue
                        chip = lax.rem((zh * depth + lane + dz) // depth, 2) * 4 + lax.rem(y + dy, 4)
                        for sibling in range(2):
                            source = refs[2 * index + sibling].at[unit]
                            owner = core if sibling == 0 else 1 - core
                            row = (chip * 2 + owner) * piece + first
                            row = pl.ds(pl.multiple_of(row, piece // 2), source.shape[0])
                            pltpu.make_async_copy(
                                source, held[part].at[slot, row], arrived[part].at[slot]
                            ).start()

    def wait(step, part):
        slot = lax.rem(step, slots)
        whole = held[part].at[slot]
        pltpu.make_async_copy(whole, whole, arrived[part].at[slot]).wait()

    def refill(step, part):
        @pl.when(step + slots < depth)
        def _():
            start(step + slots, part)

    for step in range(slots):
        for part in range(2):
            start(jnp.int32(step), part)
    return wait, refill


def forward_kernel(plan, x_ref, base_ref, *refs):
    weights, (out_ref, x_now, normed, y, *rest) = refs[: 2 * len(plan)], refs[2 * len(plan) :]
    held, arrived = rest[:2], rest[2:]
    slots = held[0].shape[0]
    split = held[0].shape[2]
    spans = (pl.ds(0, split), pl.ds(split, held[1].shape[2]))
    wait, refill = layer_copies(plan, weights, held, arrived, lambda i: i)
    x_now[...] = x_ref[...].astype(jnp.float32)

    def run_layer(layer, carry):
        values = x_now[...]
        scale = lax.rsqrt(jnp.mean(values * values, axis=-1, keepdims=True) + epsilon)
        normed[...] = (values * scale).astype(jnp.bfloat16)
        for part, columns in enumerate(spans):
            wait(layer, part)
            y[:, columns] = x_now[:, columns] + jnp.dot(
                normed[...], held[part][lax.rem(layer, slots)], preferred_element_type=jnp.float32
            )
            refill(layer, part)
        values = y[...]
        base = base_ref[layer].astype(jnp.float32)
        bound = 2.0 * jnp.sqrt(jnp.mean(values * values, axis=-1, keepdims=True) + epsilon)
        delta = jnp.clip(values - base, -bound, bound).astype(jnp.bfloat16)
        coded = (base + delta.astype(jnp.float32)).astype(jnp.bfloat16)
        out_ref[layer] = coded
        x_now[...] = coded.astype(jnp.float32)
        return carry

    lax.fori_loop(0, DEPTH, run_layer, 0)


def backward_kernel(plan, g_ref, x_ref, *refs):
    weights, (seen_ref, out_ref, g_now, back, *rest) = refs[: 2 * len(plan)], refs[2 * len(plan) :]
    held, arrived = rest[:2], rest[2:]
    slots = held[0].shape[0]
    split = held[0].shape[2]
    spans = (pl.ds(0, split), pl.ds(split, held[1].shape[2]))
    wait, refill = layer_copies(plan, weights, held, arrived, lambda i: DEPTH - 1 - i)
    g_now[...] = g_ref[...]

    def run_layer(step, carry):
        layer = DEPTH - 1 - step
        seen_ref[layer] = g_now[...]
        for part, columns in enumerate(spans):
            wait(step, part)
            product = lax.dot_general(
                g_now[:, columns], held[part][lax.rem(step, slots)], (((1,), (1,)), ((), ())),
                preferred_element_type=jnp.float32,
            )
            if part == 0:
                back[...] = product
            else:
                back[...] += product
            refill(step, part)
        values = x_ref[layer].astype(jnp.float32)
        scale = lax.rsqrt(jnp.mean(values * values, axis=-1, keepdims=True) + epsilon)
        normed = values * scale
        through = back[...]
        along = jnp.mean(normed * through, axis=-1, keepdims=True)
        sent = g_now[...].astype(jnp.float32) + scale * (through - normed * along)
        g_now[...] = sent.astype(jnp.bfloat16)
        return carry

    lax.fori_loop(0, DEPTH, run_layer, 0)
    out_ref[...] = g_now[...]


def stage_call(kernel, scratch, outs, first, second, weights):
    arrays, plan = weights
    depth, rows, width = second.shape
    vmem = pl.BlockSpec(memory_space=pltpu.VMEM)
    operands = [array for pair in arrays for array in pair]
    widths = [next(pair[0].shape[2] for pair, p in zip(arrays, plan) if p[0] == part) for part in range(2)]
    return pl.pallas_call(
        functools.partial(kernel, plan),
        in_specs=[vmem, vmem, *[pl.BlockSpec(memory_space=pl.ANY)] * len(operands)],
        out_specs=[vmem] * len(outs),
        out_shape=[jax.ShapeDtypeStruct(shape, jnp.bfloat16) for shape in outs],
        scratch_shapes=[
            *scratch,
            *[pltpu.VMEM((SLOTS, width, columns), jnp.bfloat16) for columns in widths],
            *[pltpu.SemaphoreType.DMA((SLOTS,)) for _ in widths],
        ],
        compiler_params=pltpu.CompilerParams(vmem_limit_bytes=32 * 1024 * 1024),
        cost_estimate=pl.CostEstimate(
            flops=2 * depth * rows * width * width,
            bytes_accessed=2 * depth * width * width,
            transcendentals=0,
        ),
    )(first, second, *operands)


def forward_stage(x, base, weights):
    depth, rows, width = base.shape
    scratch = [
        pltpu.VMEM((rows, width), jnp.float32),
        pltpu.VMEM((rows, width), jnp.bfloat16),
        pltpu.VMEM((rows, width), jnp.float32),
    ]
    return stage_call(forward_kernel, scratch, [(depth, rows, width)], x, base, weights)[0]


def backward_stage(g, x, weights):
    depth, rows, width = x.shape
    scratch = [pltpu.VMEM((rows, width), jnp.bfloat16), pltpu.VMEM((rows, width), jnp.float32)]
    outs = [(depth, rows, width), (rows, width)]
    return stage_call(backward_kernel, scratch, outs, g, x, weights)


def exchange(value):
    return lax.all_to_all(value, "zl", 0, 0)


def gradient_sum(normed, g):
    rows, width = normed.shape
    core, y, zh = lax.axis_index("c"), lax.axis_index("y"), lax.axis_index("zh")
    chips = lax.axis_size("zh") * lax.axis_size("y")
    piece = width // (2 * chips)
    by_core = normed.reshape(rows, chips, 2, piece)
    mine = lax.dynamic_index_in_dim(by_core, core, 2, keepdims=False).reshape(rows, -1)
    theirs = lax.dynamic_index_in_dim(by_core, 1 - core, 2, keepdims=False).reshape(rows, -1)
    left = jnp.concatenate([mine, shift(theirs, "c", 1)], axis=0)
    right = jnp.concatenate([g, shift(g, "c", 1)], axis=0)

    left = left.reshape(2 * rows, 2, 4, piece)

    def block(steps):
        picked = lax.dynamic_index_in_dim(left, lax.rem(y + steps + 4, 4), 2, keepdims=False)
        return lax.dot_general(
            picked.reshape(2 * rows, 2 * piece), right, (((0,), (0,)), ((), ())),
            preferred_element_type=jnp.float32,
        )

    half = width // 2
    far = block(2).astype(jnp.bfloat16)
    up1 = shift(far[:, :half], "y", 1)
    down1 = shift(far[:, half:], "y", -1)
    up, down, own = block(1), block(-1), block(0)
    up = jnp.concatenate([up[:, :half] + up1.astype(jnp.float32), up[:, half:]], axis=1)
    down = jnp.concatenate([down[:, :half], down[:, half:] + down1.astype(jnp.float32)], axis=1)
    up2 = shift(up.astype(jnp.bfloat16), "y", 1)
    down2 = shift(down.astype(jnp.bfloat16), "y", -1)
    total = own + up2.astype(jnp.float32) + down2.astype(jnp.float32)
    total = total.reshape(2, piece, width)
    kept = lax.dynamic_index_in_dim(total, zh, 0, keepdims=False)
    given = lax.dynamic_index_in_dim(total, 1 - zh, 0, keepdims=False).astype(jnp.bfloat16)
    return kept + shift(given, "zh", 1).astype(jnp.float32)


def local(stream_in, sample_ids, epoch_buffer, layer_weight, top_cotangent):
    stage, lane = lax.axis_index("x"), lax.axis_index("zl")
    width = stream_in.shape[1]
    rows = stream_in.shape[0] // DEPTH
    weight = gather_pieces(layer_weight[0])
    picked = jnp.take(epoch_buffer[0], sample_ids[0], axis=0)
    base = exchange(picked.reshape(DEPTH, rows, width))
    x = lax.dynamic_slice_in_dim(stream_in, lane * rows, rows, 0)
    g = lax.dynamic_slice_in_dim(top_cotangent, lane * rows, rows, 0)

    decoded = forward_stage(x, base, weight)
    for t in range(1, STAGES):
        arrived = lax.ppermute(decoded[DEPTH - 1], "x", [(t - 1, t)])
        x = jnp.where(stage == t, arrived, x)
        decoded = lax.cond(
            stage == t, lambda a, d: forward_stage(a, base, weight), lambda a, d: d, x, decoded
        )
    inputs = jnp.concatenate([x[None], decoded[: DEPTH - 1]], axis=0)

    seen, sent = backward_stage(g, inputs, weight)
    for t in range(STAGES - 2, -1, -1):
        arrived = lax.ppermute(sent, "x", [(t + 1, t)])
        g = jnp.where(stage == t, arrived, g)
        seen, sent = lax.cond(
            stage == t,
            lambda a, s, o: tuple(backward_stage(a, inputs, weight)),
            lambda a, s, o: (s, o),
            g, seen, sent,
        )

    decoded_rows = exchange(decoded).reshape(1, DEPTH * rows, width)
    input_rows = exchange(inputs).reshape(DEPTH * rows, width).astype(jnp.float32)
    scale = lax.rsqrt(jnp.mean(input_rows * input_rows, axis=-1, keepdims=True) + epsilon)
    normed = (input_rows * scale).astype(jnp.bfloat16)
    cotangents = exchange(seen).reshape(DEPTH * rows, width)
    return decoded_rows, gradient_sum(normed, cotangents)[None]


def solution(mesh):
    fine = Mesh(mesh.devices.reshape(4, 4, 2, 4, 2), ("x", "zl", "zh", "y", "c"))
    section, dp = ("x", "zl"), ("zh", "y", "c")
    in_specs = (
        P(dp, None),
        P(dp, None),
        P(section, dp, None, None),
        P(section, dp, None),
        P(dp, None),
    )
    out_specs = (P(section, dp, None), P(section, dp, None))
    return jax.shard_map(local, mesh=fine, in_specs=in_specs, out_specs=out_specs, check_vma=False)
```

```python
import functools

import jax
import jax.numpy as jnp
from jax import lax
from jax.experimental import pallas as pl
from jax.experimental.pallas import tpu as pltpu
from jax.sharding import Mesh
from jax.sharding import PartitionSpec as P

epsilon = 1e-05
STAGES = 4
DEPTH = 4
SLOTS = 2


def shift(value, axis, steps):
    count = lax.axis_size(axis)
    return lax.ppermute(value, axis, [(i, (i + steps) % count) for i in range(count)])


def shift_z(value, steps):
    lows, highs = lax.axis_size("zl"), lax.axis_size("zh")
    spot = [(z % lows) * highs + z // lows for z in range(lows * highs)]
    count = len(spot)
    return lax.ppermute(
        value, ("zl", "zh"), [(spot[z], spot[(z + steps) % count]) for z in range(count)]
    )


def base_round(picked, steps):
    lane = lax.axis_index("zl")
    target = lax.rem(lane + steps, DEPTH)
    return shift(lax.dynamic_index_in_dim(picked, target, 0, keepdims=False), "zl", steps)


def gather_pieces(shard, picked):
    split = shard.shape[1] * 11 // 16
    half = shard.shape[0] // 2
    one, two = shard[:, :split], shard[:, split:]
    pieces, waiting = [], []

    def keep(part, array, first, zs, ys):
        if array.ndim == 2:
            array = array[None]
        waiting.append([part, array, first, zs, ys])

    def swap():
        taken, waiting[:] = list(waiting), []
        swapped = [shift(entry[1], "c", 1) for entry in taken]
        return taken, swapped

    def close(taken, swapped, *arrived):
        arrived, swapped = lax.optimization_barrier((arrived, swapped))
        for entry, other in zip(taken, swapped):
            pieces.append((entry, other))
        return arrived

    def both(array, move):
        return move(array, 1), move(array, -1)

    def along_y(array, steps):
        return shift(array, "y", steps)

    def far(low, high, move):
        return move(low[..., :half, :], 1), move(high[..., half:, :], -1)

    def keep_y(part, pair, zs):
        keep(part, pair[0], 0, zs, (3,) * len(zs))
        keep(part, pair[1], 0, zs, (1,) * len(zs))

    def keep_far(part, pair, zs, ys):
        keep(part, pair[0], 0, zs, ys)
        keep(part, pair[1], half, zs, ys)

    keep(0, one, 0, (0,), (0,))
    taken, swapped = swap()
    m1, p1, low, high = close(taken, swapped, *both(one, shift_z), *both(two, along_y))
    pair1 = jnp.stack([m1, p1])
    keep(0, pair1, 0, (7, 1), (0, 0))
    taken, swapped = swap()
    m2, p2, far_low, far_high, y0_low, y0_high, base1, base3 = close(
        taken, swapped, shift_z(m1, 1), shift_z(p1, -1), *far(low, high, along_y),
        *both(one, along_y), base_round(picked, 1), base_round(picked, 3),
    )
    column = jnp.stack([two, low, high, jnp.concatenate([far_low, far_high], axis=0)])
    ys = (0, 3, 1, 2)
    pair2 = jnp.stack([m2, p2])
    keep(1, column, 0, (0,) * 4, ys)
    keep_y(0, (y0_low, y0_high), (0,))
    keep(0, pair2, 0, (6, 2), (0, 0))
    taken, swapped = swap()
    m3, p3, y1_low, y1_high, base2 = close(
        taken, swapped, shift_z(m2, 1), shift_z(p2, -1), *both(pair1, along_y), base_round(picked, 2)
    )
    pair3 = jnp.stack([m3, p3])
    keep(0, pair3, 0, (5, 3), (0, 0))
    keep_y(0, (y1_low, y1_high), (7, 1))
    taken, swapped = swap()
    c_m1, c_p1, f_low, f_high, y2_low, y2_high, y0f_low, y0f_high = close(
        taken, swapped, *both(column, shift_z), *far(m3, p3, shift_z), *both(pair2, along_y),
        *far(y0_low, y0_high, along_y),
    )
    m4 = jnp.concatenate([f_low, f_high], axis=0)
    keep(1, c_m1, 0, (7,) * 4, ys)
    keep(1, c_p1, 0, (1,) * 4, ys)
    keep(0, m4, 0, (4,), (0,))
    keep_y(0, (y2_low, y2_high), (6, 2))
    keep_far(0, (y0f_low, y0f_high), (0,), (2,))
    taken, swapped = swap()
    c_m2, c_p2, y3_low, y3_high, y1f_low, y1f_high = close(
        taken, swapped, shift_z(c_m1, 1), shift_z(c_p1, -1), *both(pair3, along_y),
        *far(y1_low, y1_high, along_y),
    )
    keep(1, c_m2, 0, (6,) * 4, ys)
    keep(1, c_p2, 0, (2,) * 4, ys)
    keep_y(0, (y3_low, y3_high), (5, 3))
    keep_far(0, (y1f_low, y1f_high), (7, 1), (2, 2))
    taken, swapped = swap()
    c_m3, c_p3, y4_low, y4_high, y2f_low, y2f_high = close(
        taken, swapped, shift_z(c_m2, 1), shift_z(c_p2, -1), *both(m4, along_y),
        *far(y2_low, y2_high, along_y),
    )
    keep(1, c_m3, 0, (5,) * 4, ys)
    keep(1, c_p3, 0, (3,) * 4, ys)
    keep_y(0, (y4_low, y4_high), (4,))
    keep_far(0, (y2f_low, y2f_high), (6, 2), (2, 2))
    taken, swapped = swap()
    c4_low, c4_high, y3f_low, y3f_high, y4f_low, y4f_high = close(
        taken, swapped, *far(c_m3, c_p3, shift_z), *far(y3_low, y3_high, along_y),
        *far(y4_low, y4_high, along_y),
    )
    keep_far(1, (c4_low, c4_high), (4,) * 4, ys)
    keep_far(0, (y3f_low, y3f_high), (5, 3), (2, 2))
    keep_far(0, (y4f_low, y4f_high), (4,), (2,))
    taken, swapped = swap()
    pieces.extend(zip(taken, swapped))

    own = lax.dynamic_index_in_dim(picked, lax.axis_index("zl"), 0, keepdims=False)
    base = jnp.stack([own, base1, base2, base3])
    arrays = [[entry[1], other] for entry, other in pieces]
    plan = [(part, first, zs, ys) for (part, _, first, zs, ys), _ in pieces]
    return (arrays, plan), base


def layer_copies(plan, refs, held, arrived, order):
    lane, zh = lax.axis_index("zl"), lax.axis_index("zh")
    y, core = lax.axis_index("y"), lax.axis_index("c")
    depth = DEPTH
    piece = held[0].shape[1] // 16
    slots = held[0].shape[0]

    def start(step, part):
        slot = lax.rem(step, slots)
        nearest = lax.rem(order(step) - lane + depth, depth)
        for offset in range(depth):

            @pl.when(nearest == offset)
            def _(offset=offset):
                for index, (kind, first, zs, ys) in enumerate(plan):
                    for unit, (dz, dy) in enumerate(zip(zs, ys)):
                        if kind != part or dz % depth != offset:
                            continue
                        chip = lax.rem((zh * depth + lane + dz) // depth, 2) * 4 + lax.rem(y + dy, 4)
                        for sibling in range(2):
                            source = refs[2 * index + sibling].at[unit]
                            owner = core if sibling == 0 else 1 - core
                            row = (chip * 2 + owner) * piece + first
                            row = pl.ds(pl.multiple_of(row, piece // 2), source.shape[0])
                            pltpu.make_async_copy(
                                source, held[part].at[slot, row], arrived[part].at[slot]
                            ).start()

    def wait(step, part):
        slot = lax.rem(step, slots)
        whole = held[part].at[slot]
        pltpu.make_async_copy(whole, whole, arrived[part].at[slot]).wait()

    return start, wait


def run_layers(copies, held, layer_start, part_product, layer_end):
    start, wait = copies
    slots = held[0].shape[0]
    split = held[0].shape[2]
    spans = (pl.ds(0, split), pl.ds(split, held[1].shape[2]))

    def iteration(count, carry):
        step = count - slots
        ready, more = step >= 0, count < DEPTH
        now = jnp.maximum(step, 0)

        @pl.when(ready)
        def _():
            layer_start(now)

        for part, columns in enumerate(spans):

            @pl.when(ready)
            def _(part=part, columns=columns):
                wait(now, part)
                part_product(part, columns, held[part].at[lax.rem(now, slots)])

            @pl.when(more)
            def _(part=part):
                start(count, part)

        @pl.when(ready)
        def _():
            layer_end(now)

        return carry

    lax.fori_loop(0, DEPTH + slots, iteration, 0)


def forward_kernel(plan, x_ref, base_ref, *refs):
    weights, rest = refs[: 2 * len(plan)], refs[2 * len(plan) :]
    in_ref, out_ref, last_ref, x_now, normed, y, *rest = rest
    held, arrived = rest[:2], rest[2:]
    lane = lax.axis_index("zl")
    copies = layer_copies(plan, weights, held, arrived, lambda i: i)
    x_now[...] = x_ref[...].astype(jnp.float32)
    in_ref[0] = x_ref[...]

    def layer_start(layer):
        values = x_now[...]
        scale = lax.rsqrt(jnp.mean(values * values, axis=-1, keepdims=True) + epsilon)
        normed[...] = (values * scale).astype(jnp.bfloat16)

    def part_product(part, columns, weight):
        y[:, columns] = x_now[:, columns] + jnp.dot(
            normed[...], weight[...], preferred_element_type=jnp.float32
        )

    def layer_end(layer):
        values = y[...]
        base = base_ref[lax.rem(lane - layer + DEPTH, DEPTH)].astype(jnp.float32)
        bound = 2.0 * jnp.sqrt(jnp.mean(values * values, axis=-1, keepdims=True) + epsilon)
        delta = jnp.clip(values - base, -bound, bound).astype(jnp.bfloat16)
        coded = (base + delta.astype(jnp.float32)).astype(jnp.bfloat16)
        out_ref[layer] = coded
        x_now[...] = coded.astype(jnp.float32)

        @pl.when(layer < DEPTH - 1)
        def _():
            in_ref[layer + 1] = coded

        @pl.when(layer == DEPTH - 1)
        def _():
            last_ref[...] = coded

    run_layers(copies, held, layer_start, part_product, layer_end)


def backward_kernel(plan, g_ref, x_ref, *refs):
    weights, (seen_ref, out_ref, g_now, back, *rest) = refs[: 2 * len(plan)], refs[2 * len(plan) :]
    held, arrived = rest[:2], rest[2:]
    copies = layer_copies(plan, weights, held, arrived, lambda i: DEPTH - 1 - i)
    g_now[...] = g_ref[...]

    def layer_start(step):
        seen_ref[DEPTH - 1 - step] = g_now[...]

    def part_product(part, columns, weight):
        product = lax.dot_general(
            g_now[:, columns], weight[...], (((1,), (1,)), ((), ())),
            preferred_element_type=jnp.float32,
        )
        if part == 0:
            back[...] = product
        else:
            back[...] += product

    def layer_end(step):
        values = x_ref[DEPTH - 1 - step].astype(jnp.float32)
        scale = lax.rsqrt(jnp.mean(values * values, axis=-1, keepdims=True) + epsilon)
        normed = values * scale
        through = back[...]
        along = jnp.mean(normed * through, axis=-1, keepdims=True)
        sent = g_now[...].astype(jnp.float32) + scale * (through - normed * along)
        g_now[...] = sent.astype(jnp.bfloat16)

    run_layers(copies, held, layer_start, part_product, layer_end)
    out_ref[...] = g_now[...]


def stage_call(kernel, scratch, outs, first, second, weights):
    arrays, plan = weights
    depth, rows, width = second.shape
    vmem = pl.BlockSpec(memory_space=pltpu.VMEM)
    operands = [array for pair in arrays for array in pair]
    widths = [next(pair[0].shape[2] for pair, p in zip(arrays, plan) if p[0] == part) for part in range(2)]
    return pl.pallas_call(
        functools.partial(kernel, plan),
        in_specs=[vmem, vmem, *[pl.BlockSpec(memory_space=pl.ANY)] * len(operands)],
        out_specs=[vmem] * len(outs),
        out_shape=[jax.ShapeDtypeStruct(shape, jnp.bfloat16) for shape in outs],
        scratch_shapes=[
            *scratch,
            *[pltpu.VMEM((SLOTS, width, columns), jnp.bfloat16) for columns in widths],
            *[pltpu.SemaphoreType.DMA((SLOTS,)) for _ in widths],
        ],
        compiler_params=pltpu.CompilerParams(vmem_limit_bytes=56 * 1024 * 1024),
        cost_estimate=pl.CostEstimate(
            flops=2 * depth * rows * width * width,
            bytes_accessed=2 * depth * width * width,
            transcendentals=0,
        ),
    )(first, second, *operands)


def forward_stage(x, base, weights):
    depth, rows, width = base.shape
    scratch = [
        pltpu.VMEM((rows, width), jnp.float32),
        pltpu.VMEM((rows, width), jnp.bfloat16),
        pltpu.VMEM((rows, width), jnp.float32),
    ]
    outs = [(depth, rows, width), (depth, rows, width), (rows, width)]
    return tuple(stage_call(forward_kernel, scratch, outs, x, base, weights))


def backward_stage(g, x, weights):
    depth, rows, width = x.shape
    scratch = [pltpu.VMEM((rows, width), jnp.bfloat16), pltpu.VMEM((rows, width), jnp.float32)]
    outs = [(depth, rows, width), (rows, width)]
    return tuple(stage_call(backward_kernel, scratch, outs, g, x, weights))


def exchange(value):
    return lax.all_to_all(value, "zl", 0, 0)


def gradient_sum(normed, g):
    rows, width = normed.shape
    core, y, zh = lax.axis_index("c"), lax.axis_index("y"), lax.axis_index("zh")
    chips = lax.axis_size("zh") * lax.axis_size("y")
    piece = width // (2 * chips)
    by_core = normed.reshape(rows, chips, 2, piece)
    mine = lax.dynamic_index_in_dim(by_core, core, 2, keepdims=False).reshape(rows, -1)
    theirs = lax.dynamic_index_in_dim(by_core, 1 - core, 2, keepdims=False).reshape(rows, -1)
    left = jnp.concatenate([mine, shift(theirs, "c", 1)], axis=0)
    right = jnp.concatenate([g, shift(g, "c", 1)], axis=0)

    left = left.reshape(2 * rows, 2, 4, piece)

    def block(steps, columns):
        picked = lax.dynamic_index_in_dim(left, lax.rem(y + steps + 4, 4), 2, keepdims=False)
        return lax.dot_general(
            picked.reshape(2 * rows, 2 * piece), columns, (((0,), (0,)), ((), ())),
            preferred_element_type=jnp.float32,
        )

    half = width // 4
    results = []
    for chunk in range(2):
        columns = right[:, chunk * 2 * half : (chunk + 1) * 2 * half]
        far = block(2, columns).astype(jnp.bfloat16)
        up1 = shift(far[:, :half], "y", 1)
        down1 = shift(far[:, half:], "y", -1)
        up, down, own = block(1, columns), block(-1, columns), block(0, columns)
        up = jnp.concatenate([up[:, :half] + up1.astype(jnp.float32), up[:, half:]], axis=1)
        down = jnp.concatenate([down[:, :half], down[:, half:] + down1.astype(jnp.float32)], axis=1)
        up2 = shift(up.astype(jnp.bfloat16), "y", 1)
        down2 = shift(down.astype(jnp.bfloat16), "y", -1)
        total = own + up2.astype(jnp.float32) + down2.astype(jnp.float32)
        total = total.reshape(2, piece, 2 * half)
        kept = lax.dynamic_index_in_dim(total, zh, 0, keepdims=False)
        given = lax.dynamic_index_in_dim(total, 1 - zh, 0, keepdims=False).astype(jnp.bfloat16)
        results.append(kept + shift(given, "zh", 1).astype(jnp.float32))
    return jnp.concatenate(results, axis=1)


def local(stream_in, sample_ids, epoch_buffer, layer_weight, top_cotangent):
    stage, lane = lax.axis_index("x"), lax.axis_index("zl")
    width = stream_in.shape[1]
    rows = stream_in.shape[0] // DEPTH
    picked = jnp.take(epoch_buffer[0], sample_ids[0], axis=0).reshape(DEPTH, rows, width)
    weight, base = gather_pieces(layer_weight[0], picked)
    x = lax.dynamic_slice_in_dim(stream_in, lane * rows, rows, 0)
    g = lax.dynamic_slice_in_dim(top_cotangent, lane * rows, rows, 0)

    state = forward_stage(x, base, weight)
    for t in range(1, STAGES):
        arrived = lax.ppermute(state[2], "x", [(t - 1, t)])
        state = lax.cond(
            stage == t, lambda a, s: forward_stage(a, base, weight), lambda a, s: s, arrived, state
        )
    inputs, decoded, _ = state

    state = backward_stage(g, inputs, weight)
    for t in range(STAGES - 2, -1, -1):
        arrived = lax.ppermute(state[1], "x", [(t + 1, t)])
        state = lax.cond(
            stage == t, lambda a, s: backward_stage(a, inputs, weight), lambda a, s: s, arrived, state
        )
    seen = state[0]

    decoded_rows = exchange(decoded).reshape(1, DEPTH * rows, width)
    input_rows = exchange(inputs).reshape(DEPTH * rows, width).astype(jnp.float32)
    scale = lax.rsqrt(jnp.mean(input_rows * input_rows, axis=-1, keepdims=True) + epsilon)
    normed = (input_rows * scale).astype(jnp.bfloat16)
    cotangents = exchange(seen).reshape(DEPTH * rows, width)
    return decoded_rows, gradient_sum(normed, cotangents)[None]


def solution(mesh):
    fine = Mesh(mesh.devices.reshape(4, 4, 2, 4, 2), ("x", "zl", "zh", "y", "c"))
    section, dp = ("x", "zl"), ("zh", "y", "c")
    in_specs = (
        P(dp, None),
        P(dp, None),
        P(section, dp, None, None),
        P(section, dp, None),
        P(dp, None),
    )
    out_specs = (P(section, dp, None), P(section, dp, None))
    return jax.shard_map(local, mesh=fine, in_specs=in_specs, out_specs=out_specs, check_vma=False)
```

```python
import functools

import jax
import jax.numpy as jnp
from jax import lax
from jax.experimental import pallas as pl
from jax.experimental.pallas import tpu as pltpu
from jax.sharding import Mesh
from jax.sharding import PartitionSpec as P

epsilon = 1e-05
STAGES = 4
DEPTH = 4
TILE = 512
SLOTS = 8
PLANE = ("zh", "zl", "y", "c")


def tile_copies(w_ref, held, arrived, order, by_rows):
    halves, depth, rows, width = w_ref.shape
    tiles, slots = width // TILE, held.shape[0]

    def start(number):
        slot = lax.rem(number, slots)
        layer = order(number // tiles)
        tile = lax.rem(number, tiles)
        if by_rows:
            inner = rows // TILE
            span = pl.ds(pl.multiple_of(lax.rem(tile, inner) * TILE, TILE), TILE)
            parts = [(w_ref.at[tile // inner, layer, span], held.at[slot])]
        else:
            span = pl.ds(pl.multiple_of(tile * TILE, TILE), TILE)
            parts = [
                (w_ref.at[half, layer, :, span], held.at[slot, pl.ds(half * rows, rows)])
                for half in range(halves)
            ]
        for source, target in parts:
            pltpu.make_async_copy(source, target, arrived.at[slot]).start()

    def wait(number):
        whole = held.at[lax.rem(number, slots)]
        pltpu.make_async_copy(whole, whole, arrived.at[lax.rem(number, slots)]).wait()

    def refill(number):
        @pl.when(number + slots < depth * tiles)
        def _():
            start(number + slots)

    for number in range(slots):
        start(jnp.int32(number))
    return wait, refill


def forward_kernel(
    x_ref, base_ref, w_ref, in_ref, out_ref, last_ref, x_now, normed, y, held, arrived
):
    depth, rows, width = base_ref.shape
    tiles, slots = width // TILE, held.shape[0]
    wait, refill = tile_copies(w_ref, held, arrived, lambda i: i, False)
    x_now[...] = x_ref[...].astype(jnp.float32)
    in_ref[0] = x_ref[...]

    def run_layer(layer, carry):
        values = x_now[...]
        scale = lax.rsqrt(jnp.mean(values * values, axis=-1, keepdims=True) + epsilon)
        normed[...] = (values * scale).astype(jnp.bfloat16)
        for tile in range(tiles):
            number = layer * tiles + tile
            wait(number)
            columns = pl.ds(tile * TILE, TILE)
            y[:, columns] = x_now[:, columns] + jnp.dot(
                normed[...], held[lax.rem(number, slots)], preferred_element_type=jnp.float32
            )
            refill(number)
        values = y[...]
        base = base_ref[layer].astype(jnp.float32)
        bound = 2.0 * jnp.sqrt(jnp.mean(values * values, axis=-1, keepdims=True) + epsilon)
        delta = jnp.clip(values - base, -bound, bound).astype(jnp.bfloat16)
        coded = (base + delta.astype(jnp.float32)).astype(jnp.bfloat16)
        out_ref[layer] = coded
        x_now[...] = coded.astype(jnp.float32)

        @pl.when(layer < depth - 1)
        def _():
            in_ref[layer + 1] = coded

        @pl.when(layer == depth - 1)
        def _():
            last_ref[...] = coded

        return carry

    lax.fori_loop(0, depth, run_layer, 0)


def backward_kernel(g_ref, x_ref, w_ref, seen_ref, out_ref, g_now, back, held, arrived):
    depth, rows, width = x_ref.shape
    tiles, slots = width // TILE, held.shape[0]
    wait, refill = tile_copies(w_ref, held, arrived, lambda i: depth - 1 - i, True)
    g_now[...] = g_ref[...]

    def run_layer(step, carry):
        layer = depth - 1 - step
        seen_ref[layer] = g_now[...]
        for tile in range(tiles):
            number = step * tiles + tile
            wait(number)
            back[:, pl.ds(tile * TILE, TILE)] = lax.dot_general(
                g_now[...], held[lax.rem(number, slots)], (((1,), (1,)), ((), ())),
                preferred_element_type=jnp.float32,
            )
            refill(number)
        values = x_ref[layer].astype(jnp.float32)
        scale = lax.rsqrt(jnp.mean(values * values, axis=-1, keepdims=True) + epsilon)
        normed = values * scale
        through = back[...]
        along = jnp.mean(normed * through, axis=-1, keepdims=True)
        sent = g_now[...].astype(jnp.float32) + scale * (through - normed * along)
        g_now[...] = sent.astype(jnp.bfloat16)
        return carry

    lax.fori_loop(0, depth, run_layer, 0)
    out_ref[...] = g_now[...]


def stage_call(kernel, tile_shape, scratch, outs, depth, rows, width):
    vmem = pl.BlockSpec(memory_space=pltpu.VMEM)
    return pl.pallas_call(
        kernel,
        in_specs=[vmem, vmem, pl.BlockSpec(memory_space=pl.ANY)],
        out_specs=[vmem] * len(outs),
        out_shape=[jax.ShapeDtypeStruct(shape, jnp.bfloat16) for shape in outs],
        scratch_shapes=[
            *scratch,
            pltpu.VMEM((SLOTS, *tile_shape), jnp.bfloat16),
            pltpu.SemaphoreType.DMA((SLOTS,)),
        ],
        compiler_params=pltpu.CompilerParams(vmem_limit_bytes=32 * 1024 * 1024),
        cost_estimate=pl.CostEstimate(
            flops=2 * depth * rows * width * width,
            bytes_accessed=2 * depth * width * width,
            transcendentals=0,
        ),
    )


def forward_stage(x, base, weight):
    depth, rows, width = base.shape
    scratch = [
        pltpu.VMEM((rows, width), jnp.float32),
        pltpu.VMEM((rows, width), jnp.bfloat16),
        pltpu.VMEM((rows, width), jnp.float32),
    ]
    outs = [(depth, rows, width), (depth, rows, width), (rows, width)]
    call = stage_call(forward_kernel, (width, TILE), scratch, outs, depth, rows, width)
    return tuple(call(x, base, weight))


def backward_stage(g, x, weight):
    depth, rows, width = x.shape
    scratch = [pltpu.VMEM((rows, width), jnp.bfloat16), pltpu.VMEM((rows, width), jnp.float32)]
    outs = [(depth, rows, width), (rows, width)]
    call = stage_call(backward_kernel, (TILE, width), scratch, outs, depth, rows, width)
    return tuple(call(g, x, weight))


def shift(value, axis, steps):
    count = lax.axis_size(axis)
    return lax.ppermute(value, axis, [(i, (i + steps) % count) for i in range(count)])


def exchange(value):
    return lax.all_to_all(value, "zl", 0, 0)


def gradient_sum(normed, g):
    rows, width = normed.shape
    core, y, zh = lax.axis_index("c"), lax.axis_index("y"), lax.axis_index("zh")
    chips = lax.axis_size("zh") * lax.axis_size("y")
    piece = width // (2 * chips)
    by_core = normed.reshape(rows, chips, 2, piece)
    mine = lax.dynamic_index_in_dim(by_core, core, 2, keepdims=False).reshape(rows, -1)
    theirs = lax.dynamic_index_in_dim(by_core, 1 - core, 2, keepdims=False).reshape(rows, -1)
    left = jnp.concatenate([mine, shift(theirs, "c", 1)], axis=0)
    right = jnp.concatenate([g, shift(g, "c", 1)], axis=0)

    left = left.reshape(2 * rows, 2, 4, piece)

    def block(steps):
        picked = lax.dynamic_index_in_dim(left, lax.rem(y + steps + 4, 4), 2, keepdims=False)
        return lax.dot_general(
            picked.reshape(2 * rows, 2 * piece), right, (((0,), (0,)), ((), ())),
            preferred_element_type=jnp.float32,
        )

    half = width // 2
    far = block(2).astype(jnp.bfloat16)
    up1 = shift(far[:, :half], "y", 1)
    down1 = shift(far[:, half:], "y", -1)
    up, down, own = block(1), block(-1), block(0)
    up = jnp.concatenate([up[:, :half] + up1.astype(jnp.float32), up[:, half:]], axis=1)
    down = jnp.concatenate([down[:, :half], down[:, half:] + down1.astype(jnp.float32)], axis=1)
    up2 = shift(up.astype(jnp.bfloat16), "y", 1)
    down2 = shift(down.astype(jnp.bfloat16), "y", -1)
    total = own + up2.astype(jnp.float32) + down2.astype(jnp.float32)
    total = total.reshape(2, piece, width)
    kept = lax.dynamic_index_in_dim(total, zh, 0, keepdims=False)
    given = lax.dynamic_index_in_dim(total, 1 - zh, 0, keepdims=False).astype(jnp.bfloat16)
    return kept + shift(given, "zh", 1).astype(jnp.float32)


def local(stream_in, sample_ids, epoch_buffer, layer_weight, top_cotangent):
    stage, lane = lax.axis_index("x"), lax.axis_index("zl")
    width = stream_in.shape[1]
    rows = stream_in.shape[0] // DEPTH
    weight = lax.all_gather(layer_weight[0], PLANE, axis=0, tiled=True)
    weight = weight.reshape(2, DEPTH, width // 2, width)
    picked = jnp.take(epoch_buffer[0], sample_ids[0], axis=0)
    base = exchange(picked.reshape(DEPTH, rows, width))
    x = lax.dynamic_slice_in_dim(stream_in, lane * rows, rows, 0)
    g = lax.dynamic_slice_in_dim(top_cotangent, lane * rows, rows, 0)

    state = forward_stage(x, base, weight)
    for t in range(1, STAGES):
        arrived = lax.ppermute(state[2], "x", [(t - 1, t)])
        state = lax.cond(
            stage == t, lambda a, s: forward_stage(a, base, weight), lambda a, s: s, arrived, state
        )
    inputs, decoded, _ = state

    state = backward_stage(g, inputs, weight)
    for t in range(STAGES - 2, -1, -1):
        arrived = lax.ppermute(state[1], "x", [(t + 1, t)])
        if t == STAGES - 2:
            held, passed, _ = lax.optimization_barrier((decoded, inputs, state[1]))
            decoded_rows, input_rows = exchange(held), exchange(passed)
            arrived, decoded_rows, input_rows = lax.optimization_barrier(
                (arrived, decoded_rows, input_rows)
            )
        state = lax.cond(
            stage == t, lambda a, s: backward_stage(a, inputs, weight), lambda a, s: s, arrived, state
        )
    seen = state[0]

    decoded_rows = decoded_rows.reshape(1, DEPTH * rows, width)
    input_rows = input_rows.reshape(DEPTH * rows, width).astype(jnp.float32)
    scale = lax.rsqrt(jnp.mean(input_rows * input_rows, axis=-1, keepdims=True) + epsilon)
    normed = (input_rows * scale).astype(jnp.bfloat16)
    cotangents = exchange(seen).reshape(DEPTH * rows, width)
    return decoded_rows, gradient_sum(normed, cotangents)[None]


def solution(mesh):
    fine = Mesh(mesh.devices.reshape(4, 4, 2, 4, 2), ("x", "zl", "zh", "y", "c"))
    section, dp = ("x", "zl"), ("zh", "y", "c")
    in_specs = (
        P(dp, None),
        P(dp, None),
        P(section, dp, None, None),
        P(section, dp, None),
        P(dp, None),
    )
    out_specs = (P(section, dp, None), P(section, dp, None))
    return jax.shard_map(local, mesh=fine, in_specs=in_specs, out_specs=out_specs, check_vma=False)
```

```python
import functools

import jax
import jax.numpy as jnp
from jax import lax
from jax.experimental import pallas as pl
from jax.experimental.pallas import tpu as pltpu
from jax.sharding import Mesh
from jax.sharding import PartitionSpec as P

epsilon = 1e-05
STAGES = 4
DEPTH = 4
TILE = 512
SLOTS = 8
PLANE = ("zh", "zl", "y", "c")


def tile_copies(w_ref, held, arrived, order):
    halves, depth, rows, width = w_ref.shape
    tiles, slots = width // TILE, held.shape[0]

    def start(number):
        slot = lax.rem(number, slots)
        layer = order(number // tiles)
        span = pl.ds(pl.multiple_of(lax.rem(number, tiles) * TILE, TILE), TILE)
        for half in range(halves):
            pltpu.make_async_copy(
                w_ref.at[half, layer, :, span],
                held.at[slot, pl.ds(half * rows, rows)],
                arrived.at[slot],
            ).start()

    def wait(number):
        whole = held.at[lax.rem(number, slots)]
        pltpu.make_async_copy(whole, whole, arrived.at[lax.rem(number, slots)]).wait()

    def refill(number):
        @pl.when(number + slots < depth * tiles)
        def _():
            start(number + slots)

    for number in range(slots):
        start(jnp.int32(number))
    return wait, refill


def forward_kernel(
    x_ref, base_ref, w_ref, in_ref, out_ref, last_ref, x_now, normed, y, held, arrived
):
    depth, rows, width = base_ref.shape
    tiles, slots = width // TILE, held.shape[0]
    wait, refill = tile_copies(w_ref, held, arrived, lambda i: i)
    x_now[...] = x_ref[...].astype(jnp.float32)
    in_ref[0] = x_ref[...]

    def run_layer(layer, carry):
        values = x_now[...]
        scale = lax.rsqrt(jnp.mean(values * values, axis=-1, keepdims=True) + epsilon)
        normed[...] = (values * scale).astype(jnp.bfloat16)
        for tile in range(tiles):
            number = layer * tiles + tile
            wait(number)
            columns = pl.ds(tile * TILE, TILE)
            y[:, columns] = x_now[:, columns] + jnp.dot(
                normed[...], held[lax.rem(number, slots)], preferred_element_type=jnp.float32
            )
            refill(number)
        values = y[...]
        base = base_ref[layer].astype(jnp.float32)
        bound = 2.0 * jnp.sqrt(jnp.mean(values * values, axis=-1, keepdims=True) + epsilon)
        delta = jnp.clip(values - base, -bound, bound).astype(jnp.bfloat16)
        coded = (base + delta.astype(jnp.float32)).astype(jnp.bfloat16)
        out_ref[layer] = coded
        x_now[...] = coded.astype(jnp.float32)

        @pl.when(layer < depth - 1)
        def _():
            in_ref[layer + 1] = coded

        @pl.when(layer == depth - 1)
        def _():
            last_ref[...] = coded

        return carry

    lax.fori_loop(0, depth, run_layer, 0)


def backward_kernel(g_ref, x_ref, w_ref, seen_ref, out_ref, g_now, back, held, arrived):
    depth, rows, width = x_ref.shape
    tiles, slots = width // TILE, held.shape[0]
    wait, refill = tile_copies(w_ref, held, arrived, lambda i: depth - 1 - i)
    g_now[...] = g_ref[...]

    def run_layer(step, carry):
        layer = depth - 1 - step
        seen_ref[layer] = g_now[...]
        for tile in range(tiles):
            number = step * tiles + tile
            wait(number)
            product = lax.dot_general(
                g_now[:, pl.ds(tile * TILE, TILE)], held[lax.rem(number, slots)],
                (((1,), (1,)), ((), ())), preferred_element_type=jnp.float32,
            )
            if tile == 0:
                back[...] = product
            else:
                back[...] += product
            refill(number)
        values = x_ref[layer].astype(jnp.float32)
        scale = lax.rsqrt(jnp.mean(values * values, axis=-1, keepdims=True) + epsilon)
        normed = values * scale
        through = back[...]
        along = jnp.mean(normed * through, axis=-1, keepdims=True)
        sent = g_now[...].astype(jnp.float32) + scale * (through - normed * along)
        g_now[...] = sent.astype(jnp.bfloat16)
        return carry

    lax.fori_loop(0, depth, run_layer, 0)
    out_ref[...] = g_now[...]


def stage_call(kernel, scratch, outs, depth, rows, width):
    vmem = pl.BlockSpec(memory_space=pltpu.VMEM)
    return pl.pallas_call(
        kernel,
        in_specs=[vmem, vmem, pl.BlockSpec(memory_space=pl.ANY)],
        out_specs=[vmem] * len(outs),
        out_shape=[jax.ShapeDtypeStruct(shape, jnp.bfloat16) for shape in outs],
        scratch_shapes=[
            *scratch,
            pltpu.VMEM((SLOTS, width, TILE), jnp.bfloat16),
            pltpu.SemaphoreType.DMA((SLOTS,)),
        ],
        compiler_params=pltpu.CompilerParams(vmem_limit_bytes=32 * 1024 * 1024),
        cost_estimate=pl.CostEstimate(
            flops=2 * depth * rows * width * width,
            bytes_accessed=2 * depth * width * width,
            transcendentals=0,
        ),
    )


def forward_stage(x, base, weight):
    depth, rows, width = base.shape
    scratch = [
        pltpu.VMEM((rows, width), jnp.float32),
        pltpu.VMEM((rows, width), jnp.bfloat16),
        pltpu.VMEM((rows, width), jnp.float32),
    ]
    outs = [(depth, rows, width), (depth, rows, width), (rows, width)]
    call = stage_call(forward_kernel, scratch, outs, depth, rows, width)
    return tuple(call(x, base, weight))


def backward_stage(g, x, weight):
    depth, rows, width = x.shape
    scratch = [pltpu.VMEM((rows, width), jnp.bfloat16), pltpu.VMEM((rows, width), jnp.float32)]
    outs = [(depth, rows, width), (rows, width)]
    call = stage_call(backward_kernel, scratch, outs, depth, rows, width)
    return tuple(call(g, x, weight))


def shift(value, axis, steps):
    count = lax.axis_size(axis)
    return lax.ppermute(value, axis, [(i, (i + steps) % count) for i in range(count)])


def exchange(value):
    lane = lax.axis_index("zl")
    blocks = []
    for steps in range(DEPTH):
        block = lax.dynamic_index_in_dim(value, lax.rem(lane + steps, DEPTH), 0, keepdims=False)
        blocks.append(shift(block, "zl", steps) if steps else block)
    return jnp.stack(blocks)


def by_sender(blocks):
    lane = lax.axis_index("zl")
    order = [lax.rem(lane - sender + DEPTH, DEPTH) for sender in range(DEPTH)]
    return jnp.stack([lax.dynamic_index_in_dim(blocks, i, 0, keepdims=False) for i in order])


def pair_rows(normed):
    rows, width = normed.shape
    core = lax.axis_index("c")
    chips = lax.axis_size("zh") * lax.axis_size("y")
    by_core = normed.reshape(rows, chips, 2, width // (2 * chips))
    mine = lax.dynamic_index_in_dim(by_core, core, 2, keepdims=False).reshape(rows, -1)
    theirs = lax.dynamic_index_in_dim(by_core, 1 - core, 2, keepdims=False).reshape(rows, -1)
    return jnp.concatenate([mine, shift(theirs, "c", 1)], axis=0)


def gradient_sum(left, g):
    rows, width = g.shape
    y, zh = lax.axis_index("y"), lax.axis_index("zh")
    chips = lax.axis_size("zh") * lax.axis_size("y")
    piece = width // (2 * chips)
    right = jnp.concatenate([g, shift(g, "c", 1)], axis=0)

    left = left.reshape(2 * rows, 2, 4, piece)

    def block(steps):
        picked = lax.dynamic_index_in_dim(left, lax.rem(y + steps + 4, 4), 2, keepdims=False)
        return lax.dot_general(
            picked.reshape(2 * rows, 2 * piece), right, (((0,), (0,)), ((), ())),
            preferred_element_type=jnp.float32,
        )

    half = width // 2
    far = block(2).astype(jnp.bfloat16)
    up1 = shift(far[:, :half], "y", 1)
    down1 = shift(far[:, half:], "y", -1)
    up, down, own = block(1), block(-1), block(0)
    up = jnp.concatenate([up[:, :half] + up1.astype(jnp.float32), up[:, half:]], axis=1)
    down = jnp.concatenate([down[:, :half], down[:, half:] + down1.astype(jnp.float32)], axis=1)
    up2 = shift(up.astype(jnp.bfloat16), "y", 1)
    down2 = shift(down.astype(jnp.bfloat16), "y", -1)
    total = own + up2.astype(jnp.float32) + down2.astype(jnp.float32)
    total = total.reshape(2, piece, width)
    kept = lax.dynamic_index_in_dim(total, zh, 0, keepdims=False)
    given = lax.dynamic_index_in_dim(total, 1 - zh, 0, keepdims=False).astype(jnp.bfloat16)
    return kept + shift(given, "zh", 1).astype(jnp.float32)


def local(stream_in, sample_ids, epoch_buffer, layer_weight, top_cotangent):
    stage, lane = lax.axis_index("x"), lax.axis_index("zl")
    width = stream_in.shape[1]
    rows = stream_in.shape[0] // DEPTH
    weight = lax.all_gather(layer_weight[0], PLANE, axis=0, tiled=True)
    weight = weight.reshape(2, DEPTH, width // 2, width)
    picked = jnp.take(epoch_buffer[0], sample_ids[0], axis=0)
    base = lax.all_to_all(picked.reshape(DEPTH, rows, width), "zl", 0, 0)
    x = lax.dynamic_slice_in_dim(stream_in, lane * rows, rows, 0)
    g = lax.dynamic_slice_in_dim(top_cotangent, lane * rows, rows, 0)

    state = forward_stage(x, base, weight)
    for t in range(1, STAGES):
        arrived = lax.ppermute(state[2], "x", [(t - 1, t)])
        state = lax.cond(
            stage == t, lambda a, s: forward_stage(a, base, weight), lambda a, s: s, arrived, state
        )
    inputs, decoded, _ = state

    state = backward_stage(g, inputs, weight)
    for t in range(STAGES - 2, -1, -1):
        arrived = lax.ppermute(state[1], "x", [(t + 1, t)])
        if t == STAGES - 2:
            held, passed, _ = lax.optimization_barrier((decoded, inputs, state[1]))
            decoded_rows, input_rows = exchange(held), exchange(passed)
        if t == 0:
            decoded_rows = by_sender(decoded_rows).reshape(1, DEPTH * rows, width)
            values = input_rows.reshape(DEPTH * rows, width).astype(jnp.float32)
            scale = lax.rsqrt(jnp.mean(values * values, axis=-1, keepdims=True) + epsilon)
            left = pair_rows((values * scale).astype(jnp.bfloat16))
            arrived, left, decoded_rows = lax.optimization_barrier((arrived, left, decoded_rows))
        state = lax.cond(
            stage == t, lambda a, s: backward_stage(a, inputs, weight), lambda a, s: s, arrived, state
        )
    cotangents = exchange(state[0]).reshape(DEPTH * rows, width)
    return decoded_rows, gradient_sum(left, cotangents)[None]


def solution(mesh):
    fine = Mesh(mesh.devices.reshape(4, 4, 2, 4, 2), ("x", "zl", "zh", "y", "c"))
    section, dp = ("x", "zl"), ("zh", "y", "c")
    in_specs = (
        P(dp, None),
        P(dp, None),
        P(section, dp, None, None),
        P(section, dp, None),
        P(dp, None),
    )
    out_specs = (P(section, dp, None), P(section, dp, None))
    return jax.shard_map(local, mesh=fine, in_specs=in_specs, out_specs=out_specs, check_vma=False)
```

```python
import functools

import jax
import jax.numpy as jnp
from jax import lax
from jax.experimental import pallas as pl
from jax.experimental.pallas import tpu as pltpu
from jax.sharding import Mesh
from jax.sharding import PartitionSpec as P

epsilon = 1e-05
STAGES = 4
DEPTH = 4
TILE = 512
SLOTS = 8
PLANE = ("zh", "zl", "y", "c")


def tile_copies(w_ref, held, arrived, order):
    halves, depth, rows, width = w_ref.shape
    tiles, slots = width // TILE, held.shape[0]

    def start(number):
        slot = lax.rem(number, slots)
        layer = order(number // tiles)
        span = pl.ds(pl.multiple_of(lax.rem(number, tiles) * TILE, TILE), TILE)
        for half in range(halves):
            pltpu.make_async_copy(
                w_ref.at[half, layer, :, span],
                held.at[slot, pl.ds(half * rows, rows)],
                arrived.at[slot],
            ).start()

    def wait(number):
        whole = held.at[lax.rem(number, slots)]
        pltpu.make_async_copy(whole, whole, arrived.at[lax.rem(number, slots)]).wait()

    def refill(number):
        @pl.when(number + slots < depth * tiles)
        def _():
            start(number + slots)

    for number in range(slots):
        start(jnp.int32(number))
    return wait, refill


def forward_kernel(
    x_ref, base_ref, w_ref, in_ref, out_ref, last_ref, x_now, normed, y, held, arrived
):
    depth, rows, width = base_ref.shape
    tiles, slots = width // TILE, held.shape[0]
    wait, refill = tile_copies(w_ref, held, arrived, lambda i: i)
    x_now[...] = x_ref[...].astype(jnp.float32)
    in_ref[0] = x_ref[...]

    def run_layer(layer, carry):
        values = x_now[...]
        scale = lax.rsqrt(jnp.mean(values * values, axis=-1, keepdims=True) + epsilon)
        normed[...] = (values * scale).astype(jnp.bfloat16)
        for tile in range(tiles):
            number = layer * tiles + tile
            wait(number)
            columns = pl.ds(tile * TILE, TILE)
            y[:, columns] = x_now[:, columns] + jnp.dot(
                normed[...], held[lax.rem(number, slots)], preferred_element_type=jnp.float32
            )
            refill(number)
        values = y[...]
        base = base_ref[layer].astype(jnp.float32)
        bound = 2.0 * jnp.sqrt(jnp.mean(values * values, axis=-1, keepdims=True) + epsilon)
        delta = jnp.clip(values - base, -bound, bound).astype(jnp.bfloat16)
        coded = (base + delta.astype(jnp.float32)).astype(jnp.bfloat16)
        out_ref[layer] = coded
        x_now[...] = coded.astype(jnp.float32)

        @pl.when(layer < depth - 1)
        def _():
            in_ref[layer + 1] = coded

        @pl.when(layer == depth - 1)
        def _():
            last_ref[...] = coded

        return carry

    lax.fori_loop(0, depth, run_layer, 0)


def backward_kernel(g_ref, x_ref, w_ref, seen_ref, out_ref, g_now, back, held, arrived):
    depth, rows, width = x_ref.shape
    tiles, slots = width // TILE, held.shape[0]
    wait, refill = tile_copies(w_ref, held, arrived, lambda i: depth - 1 - i)
    g_now[...] = g_ref[...]

    def run_layer(step, carry):
        layer = depth - 1 - step
        seen_ref[layer] = g_now[...]
        for tile in range(tiles):
            number = step * tiles + tile
            wait(number)
            product = lax.dot_general(
                g_now[:, pl.ds(tile * TILE, TILE)], held[lax.rem(number, slots)],
                (((1,), (1,)), ((), ())), preferred_element_type=jnp.float32,
            )
            if tile == 0:
                back[...] = product
            else:
                back[...] += product
            refill(number)
        values = x_ref[layer].astype(jnp.float32)
        scale = lax.rsqrt(jnp.mean(values * values, axis=-1, keepdims=True) + epsilon)
        normed = values * scale
        through = back[...]
        along = jnp.mean(normed * through, axis=-1, keepdims=True)
        sent = g_now[...].astype(jnp.float32) + scale * (through - normed * along)
        g_now[...] = sent.astype(jnp.bfloat16)
        return carry

    lax.fori_loop(0, depth, run_layer, 0)
    out_ref[...] = g_now[...]


def stage_call(kernel, scratch, outs, depth, rows, width):
    vmem = pl.BlockSpec(memory_space=pltpu.VMEM)
    return pl.pallas_call(
        kernel,
        in_specs=[vmem, vmem, pl.BlockSpec(memory_space=pl.ANY)],
        out_specs=[vmem] * len(outs),
        out_shape=[jax.ShapeDtypeStruct(shape, jnp.bfloat16) for shape in outs],
        scratch_shapes=[
            *scratch,
            pltpu.VMEM((SLOTS, width, TILE), jnp.bfloat16),
            pltpu.SemaphoreType.DMA((SLOTS,)),
        ],
        compiler_params=pltpu.CompilerParams(vmem_limit_bytes=32 * 1024 * 1024),
        cost_estimate=pl.CostEstimate(
            flops=2 * depth * rows * width * width,
            bytes_accessed=2 * depth * width * width,
            transcendentals=0,
        ),
    )


def forward_stage(x, base, weight):
    depth, rows, width = base.shape
    scratch = [
        pltpu.VMEM((rows, width), jnp.float32),
        pltpu.VMEM((rows, width), jnp.bfloat16),
        pltpu.VMEM((rows, width), jnp.float32),
    ]
    outs = [(depth, rows, width), (depth, rows, width), (rows, width)]
    call = stage_call(forward_kernel, scratch, outs, depth, rows, width)
    return tuple(call(x, base, weight))


def backward_stage(g, x, weight):
    depth, rows, width = x.shape
    scratch = [pltpu.VMEM((rows, width), jnp.bfloat16), pltpu.VMEM((rows, width), jnp.float32)]
    outs = [(depth, rows, width), (rows, width)]
    call = stage_call(backward_kernel, scratch, outs, depth, rows, width)
    return tuple(call(g, x, weight))


def shift(value, axis, steps):
    count = lax.axis_size(axis)
    return lax.ppermute(value, axis, [(i, (i + steps) % count) for i in range(count)])


def exchange(value):
    lane = lax.axis_index("zl")
    blocks = []
    for steps in range(DEPTH):
        block = lax.dynamic_index_in_dim(value, lax.rem(lane + steps, DEPTH), 0, keepdims=False)
        blocks.append(shift(block, "zl", steps) if steps else block)
    return jnp.stack(blocks)


def by_sender(blocks):
    lane = lax.axis_index("zl")
    order = [lax.rem(lane - sender + DEPTH, DEPTH) for sender in range(DEPTH)]
    return jnp.stack([lax.dynamic_index_in_dim(blocks, i, 0, keepdims=False) for i in order])


def pair_rows(normed):
    rows, width = normed.shape
    core = lax.axis_index("c")
    chips = lax.axis_size("zh") * lax.axis_size("y")
    by_core = normed.reshape(rows, chips, 2, width // (2 * chips))
    mine = lax.dynamic_index_in_dim(by_core, core, 2, keepdims=False).reshape(rows, -1)
    theirs = lax.dynamic_index_in_dim(by_core, 1 - core, 2, keepdims=False).reshape(rows, -1)
    return jnp.concatenate([mine, shift(theirs, "c", 1)], axis=0)


def gradient_sum(left, g):
    rows, width = g.shape
    y, zh = lax.axis_index("y"), lax.axis_index("zh")
    chips = lax.axis_size("zh") * lax.axis_size("y")
    piece = width // (2 * chips)
    right = jnp.concatenate([g, shift(g, "c", 1)], axis=0)

    left = left.reshape(2 * rows, 2, 4, piece)

    def block(steps):
        picked = lax.dynamic_index_in_dim(left, lax.rem(y + steps + 4, 4), 2, keepdims=False)
        return lax.dot_general(
            picked.reshape(2 * rows, 2 * piece), right, (((0,), (0,)), ((), ())),
            preferred_element_type=jnp.float32,
        )

    half = width // 2
    far = block(2).astype(jnp.bfloat16)
    up1 = shift(far[:, :half], "y", 1)
    down1 = shift(far[:, half:], "y", -1)
    up, down, own = block(1), block(-1), block(0)
    up = jnp.concatenate([up[:, :half] + up1.astype(jnp.float32), up[:, half:]], axis=1)
    down = jnp.concatenate([down[:, :half], down[:, half:] + down1.astype(jnp.float32)], axis=1)
    up2 = shift(up.astype(jnp.bfloat16), "y", 1)
    down2 = shift(down.astype(jnp.bfloat16), "y", -1)
    total = own + up2.astype(jnp.float32) + down2.astype(jnp.float32)
    total = total.reshape(2, piece, width)
    kept = lax.dynamic_index_in_dim(total, zh, 0, keepdims=False)
    given = lax.dynamic_index_in_dim(total, 1 - zh, 0, keepdims=False).astype(jnp.bfloat16)
    return kept + shift(given, "zh", 1).astype(jnp.float32)


def local(stream_in, sample_ids, epoch_buffer, layer_weight, top_cotangent):
    stage, lane = lax.axis_index("x"), lax.axis_index("zl")
    width = stream_in.shape[1]
    rows = stream_in.shape[0] // DEPTH
    weight = lax.all_gather(layer_weight[0], PLANE, axis=0, tiled=True)
    weight = weight.reshape(2, DEPTH, width // 2, width)
    picked = jnp.take(epoch_buffer[0], sample_ids[0], axis=0)
    base = lax.all_to_all(picked.reshape(DEPTH, rows, width), "zl", 0, 0)
    x = lax.dynamic_slice_in_dim(stream_in, lane * rows, rows, 0)
    g = lax.dynamic_slice_in_dim(top_cotangent, lane * rows, rows, 0)

    state = forward_stage(x, base, weight)
    for t in range(1, STAGES):
        arrived = lax.ppermute(state[2], "x", [(t - 1, t)])
        state = lax.cond(
            stage == t, lambda a, s: forward_stage(a, base, weight), lambda a, s: s, arrived, state
        )
    inputs, decoded, _ = state

    state = lax.cond(
        stage == STAGES - 1,
        lambda a, s: backward_stage(a, inputs, weight),
        lambda a, s: s,
        g, (decoded, g),
    )
    for t in range(STAGES - 2, -1, -1):
        arrived = lax.ppermute(state[1], "x", [(t + 1, t)])
        if t == STAGES - 2:
            passed, _ = lax.optimization_barrier((inputs, state[1]))
            input_rows = exchange(passed)
        if t == STAGES - 3:
            held, _ = lax.optimization_barrier((decoded, state[1]))
            decoded_rows = exchange(held)
        if t == 0:
            decoded_rows = by_sender(decoded_rows).reshape(1, DEPTH * rows, width)
            values = input_rows.reshape(DEPTH * rows, width).astype(jnp.float32)
            scale = lax.rsqrt(jnp.mean(values * values, axis=-1, keepdims=True) + epsilon)
            left = pair_rows((values * scale).astype(jnp.bfloat16))
            arrived, left, decoded_rows = lax.optimization_barrier((arrived, left, decoded_rows))
        state = lax.cond(
            stage == t, lambda a, s: backward_stage(a, inputs, weight), lambda a, s: s, arrived, state
        )
    cotangents = exchange(state[0]).reshape(DEPTH * rows, width)
    return decoded_rows, gradient_sum(left, cotangents)[None]


def solution(mesh):
    fine = Mesh(mesh.devices.reshape(4, 4, 2, 4, 2), ("x", "zl", "zh", "y", "c"))
    section, dp = ("x", "zl"), ("zh", "y", "c")
    in_specs = (
        P(dp, None),
        P(dp, None),
        P(section, dp, None, None),
        P(section, dp, None),
        P(dp, None),
    )
    out_specs = (P(section, dp, None), P(section, dp, None))
    return jax.shard_map(local, mesh=fine, in_specs=in_specs, out_specs=out_specs, check_vma=False)
```

```python
import functools

import jax
import jax.numpy as jnp
from jax import lax
from jax.experimental import pallas as pl
from jax.experimental.pallas import tpu as pltpu
from jax.sharding import Mesh
from jax.sharding import PartitionSpec as P

epsilon = 1e-05
STAGES = 4
DEPTH = 4
TILE = 512
SLOTS = 8
PLANE = ("zh", "zl", "y", "c")


def tile_copies(w_ref, held, arrived, order):
    halves, depth, rows, width = w_ref.shape
    tiles, slots = width // TILE, held.shape[0]

    def start(number):
        slot = lax.rem(number, slots)
        layer = order(number // tiles)
        span = pl.ds(pl.multiple_of(lax.rem(number, tiles) * TILE, TILE), TILE)
        for half in range(halves):
            pltpu.make_async_copy(
                w_ref.at[half, layer, :, span],
                held.at[slot, pl.ds(half * rows, rows)],
                arrived.at[slot],
            ).start()

    def wait(number):
        whole = held.at[lax.rem(number, slots)]
        pltpu.make_async_copy(whole, whole, arrived.at[lax.rem(number, slots)]).wait()

    def refill(number):
        @pl.when(number + slots < depth * tiles)
        def _():
            start(number + slots)

    for number in range(slots):
        start(jnp.int32(tiles + number))
    return wait, refill


def forward_kernel(
    x_ref, base_ref, first_ref, w_ref, in_ref, out_ref, last_ref, x_now, normed, y, held, arrived
):
    depth, rows, width = base_ref.shape
    tiles, slots = width // TILE, held.shape[0]
    wait, refill = tile_copies(w_ref, held, arrived, lambda i: i)
    x_now[...] = x_ref[...].astype(jnp.float32)
    in_ref[0] = x_ref[...]

    def run_layer(layer, carry, first=False):
        values = x_now[...]
        scale = lax.rsqrt(jnp.mean(values * values, axis=-1, keepdims=True) + epsilon)
        normed[...] = (values * scale).astype(jnp.bfloat16)
        for tile in range(tiles):
            number = layer * tiles + tile
            columns = pl.ds(tile * TILE, TILE)
            if not first:
                wait(number)
            weight = first_ref[:, columns] if first else held[lax.rem(number, slots)]
            y[:, columns] = x_now[:, columns] + jnp.dot(
                normed[...], weight, preferred_element_type=jnp.float32
            )
            if not first:
                refill(number)
        values = y[...]
        base = base_ref[layer].astype(jnp.float32)
        bound = 2.0 * jnp.sqrt(jnp.mean(values * values, axis=-1, keepdims=True) + epsilon)
        delta = jnp.clip(values - base, -bound, bound).astype(jnp.bfloat16)
        coded = (base + delta.astype(jnp.float32)).astype(jnp.bfloat16)
        out_ref[layer] = coded
        x_now[...] = coded.astype(jnp.float32)

        @pl.when(layer < depth - 1)
        def _():
            in_ref[layer + 1] = coded

        @pl.when(layer == depth - 1)
        def _():
            last_ref[...] = coded

        return carry

    run_layer(jnp.int32(0), 0, first=True)
    lax.fori_loop(1, depth, run_layer, 0)


def backward_kernel(
    g_ref, x_ref, first_ref, w_ref, seen_ref, out_ref, g_now, back, held, arrived
):
    depth, rows, width = x_ref.shape
    tiles, slots = width // TILE, held.shape[0]
    wait, refill = tile_copies(w_ref, held, arrived, lambda i: depth - 1 - i)
    g_now[...] = g_ref[...]

    def run_layer(step, carry, first=False):
        layer = depth - 1 - step
        seen_ref[layer] = g_now[...]
        for tile in range(tiles):
            number = step * tiles + tile
            columns = pl.ds(tile * TILE, TILE)
            if not first:
                wait(number)
            weight = first_ref[:, columns] if first else held[lax.rem(number, slots)]
            product = lax.dot_general(
                g_now[:, columns], weight, (((1,), (1,)), ((), ())),
                preferred_element_type=jnp.float32,
            )
            if tile == 0:
                back[...] = product
            else:
                back[...] += product
            if not first:
                refill(number)
        values = x_ref[layer].astype(jnp.float32)
        scale = lax.rsqrt(jnp.mean(values * values, axis=-1, keepdims=True) + epsilon)
        normed = values * scale
        through = back[...]
        along = jnp.mean(normed * through, axis=-1, keepdims=True)
        sent = g_now[...].astype(jnp.float32) + scale * (through - normed * along)
        g_now[...] = sent.astype(jnp.bfloat16)
        return carry

    run_layer(jnp.int32(0), 0, first=True)
    lax.fori_loop(1, depth, run_layer, 0)
    out_ref[...] = g_now[...]


def stage_call(kernel, scratch, outs, depth, rows, width):
    vmem = pl.BlockSpec(memory_space=pltpu.VMEM)
    return pl.pallas_call(
        kernel,
        in_specs=[vmem, vmem, vmem, pl.BlockSpec(memory_space=pl.ANY)],
        out_specs=[vmem] * len(outs),
        out_shape=[jax.ShapeDtypeStruct(shape, jnp.bfloat16) for shape in outs],
        scratch_shapes=[
            *scratch,
            pltpu.VMEM((SLOTS, width, TILE), jnp.bfloat16),
            pltpu.SemaphoreType.DMA((SLOTS,)),
        ],
        compiler_params=pltpu.CompilerParams(vmem_limit_bytes=32 * 1024 * 1024),
        cost_estimate=pl.CostEstimate(
            flops=2 * depth * rows * width * width,
            bytes_accessed=2 * depth * width * width,
            transcendentals=0,
        ),
    )


def forward_stage(x, base, first, weight):
    depth, rows, width = base.shape
    scratch = [
        pltpu.VMEM((rows, width), jnp.float32),
        pltpu.VMEM((rows, width), jnp.bfloat16),
        pltpu.VMEM((rows, width), jnp.float32),
    ]
    outs = [(depth, rows, width), (depth, rows, width), (rows, width)]
    call = stage_call(forward_kernel, scratch, outs, depth, rows, width)
    return tuple(call(x, base, first, weight))


def backward_stage(g, x, first, weight):
    depth, rows, width = x.shape
    scratch = [pltpu.VMEM((rows, width), jnp.bfloat16), pltpu.VMEM((rows, width), jnp.float32)]
    outs = [(depth, rows, width), (rows, width)]
    call = stage_call(backward_kernel, scratch, outs, depth, rows, width)
    return tuple(call(g, x, first, weight))


def shift(value, axis, steps):
    count = lax.axis_size(axis)
    return lax.ppermute(value, axis, [(i, (i + steps) % count) for i in range(count)])


def exchange(value):
    lane = lax.axis_index("zl")
    blocks = []
    for steps in range(DEPTH):
        block = lax.dynamic_index_in_dim(value, lax.rem(lane + steps, DEPTH), 0, keepdims=False)
        blocks.append(shift(block, "zl", steps) if steps else block)
    return jnp.stack(blocks)


def by_sender(blocks):
    lane = lax.axis_index("zl")
    order = [lax.rem(lane - sender + DEPTH, DEPTH) for sender in range(DEPTH)]
    return jnp.stack([lax.dynamic_index_in_dim(blocks, i, 0, keepdims=False) for i in order])


def pair_rows(normed):
    rows, width = normed.shape
    core = lax.axis_index("c")
    chips = lax.axis_size("zh") * lax.axis_size("y")
    by_core = normed.reshape(rows, chips, 2, width // (2 * chips))
    mine = lax.dynamic_index_in_dim(by_core, core, 2, keepdims=False).reshape(rows, -1)
    theirs = lax.dynamic_index_in_dim(by_core, 1 - core, 2, keepdims=False).reshape(rows, -1)
    return jnp.concatenate([mine, shift(theirs, "c", 1)], axis=0)


def gradient_sum(left, g):
    rows, width = g.shape
    y, zh = lax.axis_index("y"), lax.axis_index("zh")
    chips = lax.axis_size("zh") * lax.axis_size("y")
    piece = width // (2 * chips)
    right = jnp.concatenate([g, shift(g, "c", 1)], axis=0)

    left = left.reshape(2 * rows, 2, 4, piece)

    def block(steps):
        picked = lax.dynamic_index_in_dim(left, lax.rem(y + steps + 4, 4), 2, keepdims=False)
        return lax.dot_general(
            picked.reshape(2 * rows, 2 * piece), right, (((0,), (0,)), ((), ())),
            preferred_element_type=jnp.float32,
        )

    half = width // 2
    far = block(2).astype(jnp.bfloat16)
    up1 = shift(far[:, :half], "y", 1)
    down1 = shift(far[:, half:], "y", -1)
    up, down, own = block(1), block(-1), block(0)
    up = jnp.concatenate([up[:, :half] + up1.astype(jnp.float32), up[:, half:]], axis=1)
    down = jnp.concatenate([down[:, :half], down[:, half:] + down1.astype(jnp.float32)], axis=1)
    up2 = shift(up.astype(jnp.bfloat16), "y", 1)
    down2 = shift(down.astype(jnp.bfloat16), "y", -1)
    total = own + up2.astype(jnp.float32) + down2.astype(jnp.float32)
    total = total.reshape(2, piece, width)
    kept = lax.dynamic_index_in_dim(total, zh, 0, keepdims=False)
    given = lax.dynamic_index_in_dim(total, 1 - zh, 0, keepdims=False).astype(jnp.bfloat16)
    return kept + shift(given, "zh", 1).astype(jnp.float32)


def local(stream_in, sample_ids, epoch_buffer, layer_weight, top_cotangent):
    stage, lane = lax.axis_index("x"), lax.axis_index("zl")
    width = stream_in.shape[1]
    rows = stream_in.shape[0] // DEPTH
    weight = lax.all_gather(layer_weight[0], PLANE, axis=0, tiled=True)
    weight = weight.reshape(2, DEPTH, width // 2, width)
    picked = jnp.take(epoch_buffer[0], sample_ids[0], axis=0)
    base = lax.all_to_all(picked.reshape(DEPTH, rows, width), "zl", 0, 0)
    x = lax.dynamic_slice_in_dim(stream_in, lane * rows, rows, 0)
    g = lax.dynamic_slice_in_dim(top_cotangent, lane * rows, rows, 0)

    first = weight[:, 0].reshape(width, width)
    state = forward_stage(x, base, first, weight)
    index, _ = lax.optimization_barrier((jnp.int32(DEPTH - 1), state[2]))
    final = lax.dynamic_index_in_dim(weight, index, 1, keepdims=False).reshape(width, width)
    for t in range(1, STAGES):
        arrived = lax.ppermute(state[2], "x", [(t - 1, t)])
        state = lax.cond(
            stage == t, lambda a, s: forward_stage(a, base, first, weight), lambda a, s: s, arrived, state
        )
    inputs, decoded, _ = state

    state = lax.cond(
        stage == STAGES - 1,
        lambda a, s: backward_stage(a, inputs, final, weight),
        lambda a, s: s,
        g, (decoded, g),
    )
    for t in range(STAGES - 2, -1, -1):
        arrived = lax.ppermute(state[1], "x", [(t + 1, t)])
        if t == STAGES - 2:
            passed, _ = lax.optimization_barrier((inputs, state[1]))
            input_rows = exchange(passed)
        if t == STAGES - 3:
            held, _ = lax.optimization_barrier((decoded, state[1]))
            decoded_rows = exchange(held)
        if t == 0:
            decoded_rows = by_sender(decoded_rows).reshape(1, DEPTH * rows, width)
            values = input_rows.reshape(DEPTH * rows, width).astype(jnp.float32)
            scale = lax.rsqrt(jnp.mean(values * values, axis=-1, keepdims=True) + epsilon)
            left = pair_rows((values * scale).astype(jnp.bfloat16))
            arrived, left, decoded_rows = lax.optimization_barrier((arrived, left, decoded_rows))
        state = lax.cond(
            stage == t, lambda a, s: backward_stage(a, inputs, final, weight), lambda a, s: s, arrived, state
        )
    cotangents = exchange(state[0]).reshape(DEPTH * rows, width)
    return decoded_rows, gradient_sum(left, cotangents)[None]


def solution(mesh):
    fine = Mesh(mesh.devices.reshape(4, 4, 2, 4, 2), ("x", "zl", "zh", "y", "c"))
    section, dp = ("x", "zl"), ("zh", "y", "c")
    in_specs = (
        P(dp, None),
        P(dp, None),
        P(section, dp, None, None),
        P(section, dp, None),
        P(dp, None),
    )
    out_specs = (P(section, dp, None), P(section, dp, None))
    return jax.shard_map(local, mesh=fine, in_specs=in_specs, out_specs=out_specs, check_vma=False)
```

```python
import functools

import jax
import jax.numpy as jnp
from jax import lax
from jax.experimental import pallas as pl
from jax.experimental.pallas import tpu as pltpu
from jax.sharding import Mesh
from jax.sharding import PartitionSpec as P

epsilon = 1e-05
STAGES = 4
DEPTH = 4
TILE = 512
SLOTS = 8
PLANE = ("zh", "zl", "y", "c")


def tile_copies(w_ref, held, arrived, order):
    halves, depth, rows, width = w_ref.shape
    tiles, slots = width // TILE, held.shape[0]

    def start(number):
        slot = lax.rem(number, slots)
        layer = order(number // tiles)
        span = pl.ds(pl.multiple_of(lax.rem(number, tiles) * TILE, TILE), TILE)
        for half in range(halves):
            pltpu.make_async_copy(
                w_ref.at[half, layer, :, span],
                held.at[slot, pl.ds(half * rows, rows)],
                arrived.at[slot],
            ).start()

    def wait(number):
        whole = held.at[lax.rem(number, slots)]
        pltpu.make_async_copy(whole, whole, arrived.at[lax.rem(number, slots)]).wait()

    def refill(number):
        @pl.when(number + slots < depth * tiles)
        def _():
            start(number + slots)

    for number in range(slots):
        start(jnp.int32(number))
    return wait, refill


def forward_kernel(
    x_ref, base_ref, w_ref, in_ref, out_ref, last_ref, x_now, normed, y, held, arrived
):
    depth, rows, width = base_ref.shape
    tiles, slots = width // TILE, held.shape[0]
    wait, refill = tile_copies(w_ref, held, arrived, lambda i: i)
    x_now[...] = x_ref[...].astype(jnp.float32)
    in_ref[0] = x_ref[...]

    def run_layer(layer, carry):
        values = x_now[...]
        scale = lax.rsqrt(jnp.mean(values * values, axis=-1, keepdims=True) + epsilon)
        normed[...] = (values * scale).astype(jnp.bfloat16)
        for tile in range(tiles):
            number = layer * tiles + tile
            wait(number)
            columns = pl.ds(tile * TILE, TILE)
            y[:, columns] = x_now[:, columns] + jnp.dot(
                normed[...], held[lax.rem(number, slots)], preferred_element_type=jnp.float32
            )
            refill(number)
        values = y[...]
        base = base_ref[layer].astype(jnp.float32)
        bound = 2.0 * jnp.sqrt(jnp.mean(values * values, axis=-1, keepdims=True) + epsilon)
        delta = jnp.clip(values - base, -bound, bound).astype(jnp.bfloat16)
        coded = (base + delta.astype(jnp.float32)).astype(jnp.bfloat16)
        out_ref[layer] = coded
        x_now[...] = coded.astype(jnp.float32)

        @pl.when(layer < depth - 1)
        def _():
            in_ref[layer + 1] = coded

        @pl.when(layer == depth - 1)
        def _():
            last_ref[...] = coded

        return carry

    lax.fori_loop(0, depth, run_layer, 0)


def backward_kernel(g_ref, x_ref, w_ref, seen_ref, out_ref, g_now, back, held, arrived):
    depth, rows, width = x_ref.shape
    tiles, slots = width // TILE, held.shape[0]
    wait, refill = tile_copies(w_ref, held, arrived, lambda i: depth - 1 - i)
    g_now[...] = g_ref[...]

    def run_layer(step, carry):
        layer = depth - 1 - step
        seen_ref[layer] = g_now[...]
        for tile in range(tiles):
            number = step * tiles + tile
            wait(number)
            product = lax.dot_general(
                g_now[:, pl.ds(tile * TILE, TILE)], held[lax.rem(number, slots)],
                (((1,), (1,)), ((), ())), preferred_element_type=jnp.float32,
            )
            if tile == 0:
                back[...] = product
            else:
                back[...] += product
            refill(number)
        values = x_ref[layer].astype(jnp.float32)
        scale = lax.rsqrt(jnp.mean(values * values, axis=-1, keepdims=True) + epsilon)
        normed = values * scale
        through = back[...]
        along = jnp.mean(normed * through, axis=-1, keepdims=True)
        sent = g_now[...].astype(jnp.float32) + scale * (through - normed * along)
        g_now[...] = sent.astype(jnp.bfloat16)
        return carry

    lax.fori_loop(0, depth, run_layer, 0)
    out_ref[...] = g_now[...]


def stage_call(kernel, scratch, outs, depth, rows, width):
    vmem = pl.BlockSpec(memory_space=pltpu.VMEM)
    return pl.pallas_call(
        kernel,
        in_specs=[vmem, vmem, pl.BlockSpec(memory_space=pl.ANY)],
        out_specs=[vmem] * len(outs),
        out_shape=[jax.ShapeDtypeStruct(shape, jnp.bfloat16) for shape in outs],
        scratch_shapes=[
            *scratch,
            pltpu.VMEM((SLOTS, width, TILE), jnp.bfloat16),
            pltpu.SemaphoreType.DMA((SLOTS,)),
        ],
        compiler_params=pltpu.CompilerParams(vmem_limit_bytes=32 * 1024 * 1024),
        cost_estimate=pl.CostEstimate(
            flops=2 * depth * rows * width * width,
            bytes_accessed=2 * depth * width * width,
            transcendentals=0,
        ),
    )


def forward_stage(x, base, weight):
    depth, rows, width = base.shape
    scratch = [
        pltpu.VMEM((rows, width), jnp.float32),
        pltpu.VMEM((rows, width), jnp.bfloat16),
        pltpu.VMEM((rows, width), jnp.float32),
    ]
    outs = [(depth, rows, width), (depth, rows, width), (rows, width)]
    call = stage_call(forward_kernel, scratch, outs, depth, rows, width)
    return tuple(call(x, base, weight))


def backward_stage(g, x, weight):
    depth, rows, width = x.shape
    scratch = [pltpu.VMEM((rows, width), jnp.bfloat16), pltpu.VMEM((rows, width), jnp.float32)]
    outs = [(depth, rows, width), (rows, width)]
    call = stage_call(backward_kernel, scratch, outs, depth, rows, width)
    return tuple(call(g, x, weight))


def shift(value, axis, steps):
    count = lax.axis_size(axis)
    return lax.ppermute(value, axis, [(i, (i + steps) % count) for i in range(count)])


def exchange(value):
    lane = lax.axis_index("zl")
    blocks = []
    for steps in range(DEPTH):
        block = lax.dynamic_index_in_dim(value, lax.rem(lane + steps, DEPTH), 0, keepdims=False)
        blocks.append(shift(block, "zl", steps) if steps else block)
    return jnp.stack(blocks)


def by_sender(blocks):
    lane = lax.axis_index("zl")
    order = [lax.rem(lane - sender + DEPTH, DEPTH) for sender in range(DEPTH)]
    return jnp.stack([lax.dynamic_index_in_dim(blocks, i, 0, keepdims=False) for i in order])


def pair_rows(normed):
    rows, width = normed.shape
    core = lax.axis_index("c")
    chips = lax.axis_size("zh") * lax.axis_size("y")
    by_core = normed.reshape(rows, chips, 2, width // (2 * chips))
    mine = lax.dynamic_index_in_dim(by_core, core, 2, keepdims=False).reshape(rows, -1)
    theirs = lax.dynamic_index_in_dim(by_core, 1 - core, 2, keepdims=False).reshape(rows, -1)
    return jnp.concatenate([mine, shift(theirs, "c", 1)], axis=0)


def gradient_sum(left, g):
    rows, width = g.shape
    y, zh = lax.axis_index("y"), lax.axis_index("zh")
    chips = lax.axis_size("zh") * lax.axis_size("y")
    piece = width // (2 * chips)
    right = jnp.concatenate([g, shift(g, "c", 1)], axis=0)

    def product(columns, block):
        return lax.dot_general(
            columns, block, (((0,), (0,)), ((), ())), preferred_element_type=jnp.float32
        )

    def round_y(block):
        far = block(2).astype(jnp.bfloat16)
        half = far.shape[1] // 2
        up1 = shift(far[:, :half], "y", 1)
        down1 = shift(far[:, half:], "y", -1)
        up, down, own = block(1), block(-1), block(0)
        up = jnp.concatenate([up[:, :half] + up1.astype(jnp.float32), up[:, half:]], axis=1)
        down = jnp.concatenate([down[:, :half], down[:, half:] + down1.astype(jnp.float32)], axis=1)
        up2 = shift(up.astype(jnp.bfloat16), "y", 1)
        down2 = shift(down.astype(jnp.bfloat16), "y", -1)
        return own + up2.astype(jnp.float32) + down2.astype(jnp.float32)

    def pick_y(array, steps, axis):
        return lax.dynamic_index_in_dim(array, lax.rem(y + steps + 4, 4), axis, keepdims=False)

    split = width * 3 // 4
    left = left.reshape(2 * rows, 2, 4, piece)

    def plane(which):
        picked = lax.dynamic_index_in_dim(left, which, 1, keepdims=False)
        return product(picked.reshape(2 * rows, 4 * piece), right[:, split:])

    passed = shift(plane(1 - zh).astype(jnp.bfloat16), "zh", 1)

    def block(steps):
        picked = pick_y(left, steps, 2).reshape(2 * rows, 2 * piece)
        return product(picked, right[:, :split])

    total = round_y(block).reshape(2, piece, split)
    kept = lax.dynamic_index_in_dim(total, zh, 0, keepdims=False)
    given = lax.dynamic_index_in_dim(total, 1 - zh, 0, keepdims=False).astype(jnp.bfloat16)
    one = kept + shift(given, "zh", 1).astype(jnp.float32)

    both = (plane(zh) + passed.astype(jnp.float32)).reshape(4, piece, width - split)
    two = round_y(lambda steps: pick_y(both, steps, 0))
    return jnp.concatenate([one, two], axis=1)


def local(stream_in, sample_ids, epoch_buffer, layer_weight, top_cotangent):
    stage, lane = lax.axis_index("x"), lax.axis_index("zl")
    width = stream_in.shape[1]
    rows = stream_in.shape[0] // DEPTH
    weight = lax.all_gather(layer_weight[0], PLANE, axis=0, tiled=True)
    weight = weight.reshape(2, DEPTH, width // 2, width)
    picked = jnp.take(epoch_buffer[0], sample_ids[0], axis=0)
    base = lax.all_to_all(picked.reshape(DEPTH, rows, width), "zl", 0, 0)
    x = lax.dynamic_slice_in_dim(stream_in, lane * rows, rows, 0)
    g = lax.dynamic_slice_in_dim(top_cotangent, lane * rows, rows, 0)

    state = forward_stage(x, base, weight)
    for t in range(1, STAGES):
        arrived = lax.ppermute(state[2], "x", [(t - 1, t)])
        state = lax.cond(
            stage == t, lambda a, s: forward_stage(a, base, weight), lambda a, s: s, arrived, state
        )
    inputs, decoded, _ = state

    state = lax.cond(
        stage == STAGES - 1,
        lambda a, s: backward_stage(a, inputs, weight),
        lambda a, s: s,
        g, (decoded, g),
    )
    for t in range(STAGES - 2, -1, -1):
        arrived = lax.ppermute(state[1], "x", [(t + 1, t)])
        if t == STAGES - 2:
            passed, _ = lax.optimization_barrier((inputs, state[1]))
            input_rows = exchange(passed)
        if t == STAGES - 3:
            held, _ = lax.optimization_barrier((decoded, state[1]))
            decoded_rows = exchange(held)
        if t == 0:
            decoded_rows = by_sender(decoded_rows).reshape(1, DEPTH * rows, width)
            values = input_rows.reshape(DEPTH * rows, width).astype(jnp.float32)
            scale = lax.rsqrt(jnp.mean(values * values, axis=-1, keepdims=True) + epsilon)
            left = pair_rows((values * scale).astype(jnp.bfloat16))
            arrived, left, decoded_rows = lax.optimization_barrier((arrived, left, decoded_rows))
        state = lax.cond(
            stage == t, lambda a, s: backward_stage(a, inputs, weight), lambda a, s: s, arrived, state
        )
    cotangents = exchange(state[0]).reshape(DEPTH * rows, width)
    return decoded_rows, gradient_sum(left, cotangents)[None]


def solution(mesh):
    fine = Mesh(mesh.devices.reshape(4, 4, 2, 4, 2), ("x", "zl", "zh", "y", "c"))
    section, dp = ("x", "zl"), ("zh", "y", "c")
    in_specs = (
        P(dp, None),
        P(dp, None),
        P(section, dp, None, None),
        P(section, dp, None),
        P(dp, None),
    )
    out_specs = (P(section, dp, None), P(section, dp, None))
    return jax.shard_map(local, mesh=fine, in_specs=in_specs, out_specs=out_specs, check_vma=False)
```

```python
import functools

import jax
import jax.numpy as jnp
from jax import lax
from jax.experimental import pallas as pl
from jax.experimental.pallas import tpu as pltpu
from jax.sharding import Mesh
from jax.sharding import PartitionSpec as P

epsilon = 1e-05
STAGES = 4
DEPTH = 4
TILE = 512
SLOTS = 8
PLANE = ("zh", "zl", "y", "c")


def tile_copies(w_ref, held, arrived, order, resident=0):
    halves, depth, rows, width = w_ref.shape
    tiles, slots = width // TILE, held.shape[0]

    def slot_of(number):
        return lax.rem(number + resident // 2, slots)

    def start(number):
        slot = slot_of(number)
        layer = order(number // tiles)
        span = pl.ds(pl.multiple_of(lax.rem(number, tiles) * TILE, TILE), TILE)
        for half in range(halves):
            pltpu.make_async_copy(
                w_ref.at[half, layer, :, span],
                held.at[slot, pl.ds(half * rows, rows)],
                arrived.at[slot],
            ).start()

    def wait(number):
        @pl.when(number >= resident)
        def _():
            whole = held.at[slot_of(number)]
            pltpu.make_async_copy(whole, whole, arrived.at[slot_of(number)]).wait()

    def refill(number):
        @pl.when(number + slots < depth * tiles)
        def _():
            start(number + slots)

    for number in range(resident, slots):
        start(jnp.int32(number))
    return wait, refill, slot_of


def forward_kernel(
    x_ref, base_ref, w_ref, in_ref, out_ref, last_ref, x_now, normed, y, held, arrived
):
    depth, rows, width = base_ref.shape
    tiles, slots = width // TILE, held.shape[0]
    wait, refill, slot_of = tile_copies(w_ref, held, arrived, lambda i: i)
    x_now[...] = x_ref[...].astype(jnp.float32)
    in_ref[0] = x_ref[...]

    def run_layer(layer, carry):
        values = x_now[...]
        scale = lax.rsqrt(jnp.mean(values * values, axis=-1, keepdims=True) + epsilon)
        normed[...] = (values * scale).astype(jnp.bfloat16)
        for tile in range(tiles):
            number = layer * tiles + tile
            wait(number)
            columns = pl.ds(tile * TILE, TILE)
            y[:, columns] = x_now[:, columns] + jnp.dot(
                normed[...], held[slot_of(number)], preferred_element_type=jnp.float32
            )
            refill(number)
        values = y[...]
        base = base_ref[layer].astype(jnp.float32)
        bound = 2.0 * jnp.sqrt(jnp.mean(values * values, axis=-1, keepdims=True) + epsilon)
        delta = jnp.clip(values - base, -bound, bound).astype(jnp.bfloat16)
        coded = (base + delta.astype(jnp.float32)).astype(jnp.bfloat16)
        out_ref[layer] = coded
        x_now[...] = coded.astype(jnp.float32)

        @pl.when(layer < depth - 1)
        def _():
            in_ref[layer + 1] = coded

        @pl.when(layer == depth - 1)
        def _():
            last_ref[...] = coded

        return carry

    lax.fori_loop(0, depth, run_layer, 0)


def backward_kernel(
    g_ref, x_ref, w_ref, seen_ref, out_ref, g_now, back, held, arrived, resident=0
):
    depth, rows, width = x_ref.shape
    tiles, slots = width // TILE, held.shape[0]
    wait, refill, slot_of = tile_copies(
        w_ref, held, arrived, lambda i: depth - 1 - i, resident
    )
    g_now[...] = g_ref[...]

    def run_layer(step, carry):
        layer = depth - 1 - step
        seen_ref[layer] = g_now[...]
        for tile in range(tiles):
            number = step * tiles + tile
            wait(number)
            product = lax.dot_general(
                g_now[:, pl.ds(tile * TILE, TILE)], held[slot_of(number)],
                (((1,), (1,)), ((), ())), preferred_element_type=jnp.float32,
            )
            if tile == 0:
                back[...] = product
            else:
                back[...] += product
            refill(number)
        values = x_ref[layer].astype(jnp.float32)
        scale = lax.rsqrt(jnp.mean(values * values, axis=-1, keepdims=True) + epsilon)
        normed = values * scale
        through = back[...]
        along = jnp.mean(normed * through, axis=-1, keepdims=True)
        sent = g_now[...].astype(jnp.float32) + scale * (through - normed * along)
        g_now[...] = sent.astype(jnp.bfloat16)
        return carry

    lax.fori_loop(0, depth, run_layer, 0)
    out_ref[...] = g_now[...]


def turn_kernel(
    x_ref, base_ref, w_ref, g_ref, in_ref, out_ref, seen_ref, sent_ref,
    x_now, normed, y, g_now, back, held, arrived,
):
    forward_kernel(
        x_ref, base_ref, w_ref, in_ref, out_ref, sent_ref, x_now, normed, y, held, arrived
    )
    backward_kernel(
        g_ref, in_ref, w_ref, seen_ref, sent_ref, g_now, back, held, arrived, resident=SLOTS
    )


def stage_call(kernel, scratch, outs, depth, rows, width, more=()):
    vmem = pl.BlockSpec(memory_space=pltpu.VMEM)
    return pl.pallas_call(
        kernel,
        in_specs=[vmem, vmem, pl.BlockSpec(memory_space=pl.ANY), *more],
        out_specs=[vmem] * len(outs),
        out_shape=[jax.ShapeDtypeStruct(shape, jnp.bfloat16) for shape in outs],
        scratch_shapes=[
            *scratch,
            pltpu.VMEM((SLOTS, width, TILE), jnp.bfloat16),
            pltpu.SemaphoreType.DMA((SLOTS,)),
        ],
        compiler_params=pltpu.CompilerParams(vmem_limit_bytes=32 * 1024 * 1024),
        cost_estimate=pl.CostEstimate(
            flops=2 * depth * rows * width * width,
            bytes_accessed=2 * depth * width * width,
            transcendentals=0,
        ),
    )


def forward_stage(x, base, weight):
    depth, rows, width = base.shape
    scratch = [
        pltpu.VMEM((rows, width), jnp.float32),
        pltpu.VMEM((rows, width), jnp.bfloat16),
        pltpu.VMEM((rows, width), jnp.float32),
    ]
    outs = [(depth, rows, width), (depth, rows, width), (rows, width)]
    call = stage_call(forward_kernel, scratch, outs, depth, rows, width)
    return tuple(call(x, base, weight))


def backward_stage(g, x, weight):
    depth, rows, width = x.shape
    scratch = [pltpu.VMEM((rows, width), jnp.bfloat16), pltpu.VMEM((rows, width), jnp.float32)]
    outs = [(depth, rows, width), (rows, width)]
    call = stage_call(backward_kernel, scratch, outs, depth, rows, width)
    return tuple(call(g, x, weight))


def turn_stage(x, base, weight, g):
    depth, rows, width = base.shape
    wide, narrow = pltpu.VMEM((rows, width), jnp.float32), pltpu.VMEM((rows, width), jnp.bfloat16)
    stack = (depth, rows, width)
    call = stage_call(
        turn_kernel, [wide, narrow, wide, narrow, wide], [stack, stack, stack, (rows, width)],
        depth, rows, width, more=[pl.BlockSpec(memory_space=pltpu.VMEM)],
    )
    return tuple(call(x, base, weight, g))


def shift(value, axis, steps):
    count = lax.axis_size(axis)
    return lax.ppermute(value, axis, [(i, (i + steps) % count) for i in range(count)])


def exchange(value):
    lane = lax.axis_index("zl")
    blocks = []
    for steps in range(DEPTH):
        block = lax.dynamic_index_in_dim(value, lax.rem(lane + steps, DEPTH), 0, keepdims=False)
        blocks.append(shift(block, "zl", steps) if steps else block)
    return jnp.stack(blocks)


def by_sender(blocks):
    lane = lax.axis_index("zl")
    order = [lax.rem(lane - sender + DEPTH, DEPTH) for sender in range(DEPTH)]
    return jnp.stack([lax.dynamic_index_in_dim(blocks, i, 0, keepdims=False) for i in order])


def pair_rows(normed):
    rows, width = normed.shape
    core = lax.axis_index("c")
    chips = lax.axis_size("zh") * lax.axis_size("y")
    by_core = normed.reshape(rows, chips, 2, width // (2 * chips))
    mine = lax.dynamic_index_in_dim(by_core, core, 2, keepdims=False).reshape(rows, -1)
    theirs = lax.dynamic_index_in_dim(by_core, 1 - core, 2, keepdims=False).reshape(rows, -1)
    return jnp.concatenate([mine, shift(theirs, "c", 1)], axis=0)


def gradient_sum(left, g):
    rows, width = g.shape
    y, zh = lax.axis_index("y"), lax.axis_index("zh")
    chips = lax.axis_size("zh") * lax.axis_size("y")
    piece = width // (2 * chips)
    right = jnp.concatenate([g, shift(g, "c", 1)], axis=0)

    def product(columns, block):
        return lax.dot_general(
            columns, block, (((0,), (0,)), ((), ())), preferred_element_type=jnp.float32
        )

    def round_y(block):
        far = block(2).astype(jnp.bfloat16)
        half = far.shape[1] // 2
        up1 = shift(far[:, :half], "y", 1)
        down1 = shift(far[:, half:], "y", -1)
        up, down, own = block(1), block(-1), block(0)
        up = jnp.concatenate([up[:, :half] + up1.astype(jnp.float32), up[:, half:]], axis=1)
        down = jnp.concatenate([down[:, :half], down[:, half:] + down1.astype(jnp.float32)], axis=1)
        up2 = shift(up.astype(jnp.bfloat16), "y", 1)
        down2 = shift(down.astype(jnp.bfloat16), "y", -1)
        return own + up2.astype(jnp.float32) + down2.astype(jnp.float32)

    def pick_y(array, steps, axis):
        return lax.dynamic_index_in_dim(array, lax.rem(y + steps + 4, 4), axis, keepdims=False)

    split = width * 3 // 4
    left = left.reshape(2 * rows, 2, 4, piece)

    def plane(which):
        picked = lax.dynamic_index_in_dim(left, which, 1, keepdims=False)
        return product(picked.reshape(2 * rows, 4 * piece), right[:, split:])

    passed = shift(plane(1 - zh).astype(jnp.bfloat16), "zh", 1)

    def block(steps):
        picked = pick_y(left, steps, 2).reshape(2 * rows, 2 * piece)
        return product(picked, right[:, :split])

    total = round_y(block).reshape(2, piece, split)
    kept = lax.dynamic_index_in_dim(total, zh, 0, keepdims=False)
    given = lax.dynamic_index_in_dim(total, 1 - zh, 0, keepdims=False).astype(jnp.bfloat16)
    one = kept + shift(given, "zh", 1).astype(jnp.float32)

    both = (plane(zh) + passed.astype(jnp.float32)).reshape(4, piece, width - split)
    two = round_y(lambda steps: pick_y(both, steps, 0))
    return jnp.concatenate([one, two], axis=1)


def local(stream_in, sample_ids, epoch_buffer, layer_weight, top_cotangent):
    stage, lane = lax.axis_index("x"), lax.axis_index("zl")
    width = stream_in.shape[1]
    rows = stream_in.shape[0] // DEPTH
    weight = lax.all_gather(layer_weight[0], PLANE, axis=0, tiled=True)
    weight = weight.reshape(2, DEPTH, width // 2, width)
    picked = jnp.take(epoch_buffer[0], sample_ids[0], axis=0)
    base = lax.all_to_all(picked.reshape(DEPTH, rows, width), "zl", 0, 0)
    x = lax.dynamic_slice_in_dim(stream_in, lane * rows, rows, 0)
    g = lax.dynamic_slice_in_dim(top_cotangent, lane * rows, rows, 0)

    state = forward_stage(x, base, weight)
    for t in range(1, STAGES - 1):
        arrived = lax.ppermute(state[2], "x", [(t - 1, t)])
        state = lax.cond(
            stage == t, lambda a, s: forward_stage(a, base, weight), lambda a, s: s, arrived, state
        )
    arrived = lax.ppermute(state[2], "x", [(STAGES - 2, STAGES - 1)])
    inputs, decoded, *state = lax.cond(
        stage == STAGES - 1,
        lambda a, s: turn_stage(a, base, weight, g),
        lambda a, s: (s[0], s[1], s[1], g),
        arrived, state,
    )
    state = tuple(state)

    for t in range(STAGES - 2, -1, -1):
        arrived = lax.ppermute(state[1], "x", [(t + 1, t)])
        if t == STAGES - 2:
            passed, _ = lax.optimization_barrier((inputs, state[1]))
            input_rows = exchange(passed)
        if t == STAGES - 3:
            held, _ = lax.optimization_barrier((decoded, state[1]))
            decoded_rows = exchange(held)
        if t == 0:
            decoded_rows = by_sender(decoded_rows).reshape(1, DEPTH * rows, width)
            values = input_rows.reshape(DEPTH * rows, width).astype(jnp.float32)
            scale = lax.rsqrt(jnp.mean(values * values, axis=-1, keepdims=True) + epsilon)
            left = pair_rows((values * scale).astype(jnp.bfloat16))
            arrived, left, decoded_rows = lax.optimization_barrier((arrived, left, decoded_rows))
        state = lax.cond(
            stage == t, lambda a, s: backward_stage(a, inputs, weight), lambda a, s: s, arrived, state
        )
    cotangents = exchange(state[0]).reshape(DEPTH * rows, width)
    return decoded_rows, gradient_sum(left, cotangents)[None]


def solution(mesh):
    fine = Mesh(mesh.devices.reshape(4, 4, 2, 4, 2), ("x", "zl", "zh", "y", "c"))
    section, dp = ("x", "zl"), ("zh", "y", "c")
    in_specs = (
        P(dp, None),
        P(dp, None),
        P(section, dp, None, None),
        P(section, dp, None),
        P(dp, None),
    )
    out_specs = (P(section, dp, None), P(section, dp, None))
    return jax.shard_map(local, mesh=fine, in_specs=in_specs, out_specs=out_specs, check_vma=False)
```
